512 devices in a mesh: gx: 8 (over z_hi, core), gy: 16 (over x, z_lo), dev: 4 (over y).
Axes of the slice: x: 4, y: 4, z: 16 (z_hi: 4, z_lo: 4; z = z_hi * 4 + z_lo), core: 2. Of those that a mesh axis runs over, the one named last changes fastest.
Arguments:
- volume: bfloat16 [16, 16, 128, 4096], P(None, None, ('gx', 'dev'), 'gy'), may hold values from -6 to 6
- w_first: bfloat16 [16, 16, 3, 3, 3], replicated, may hold values from -0.4375 to 0.4375
- w_second: bfloat16 [16, 16, 3, 3, 3], replicated, may hold values from -0.4375 to 0.4375
- w_third: bfloat16 [32, 16, 3, 3, 3], replicated, may hold values from -0.4375 to 0.4375
- w_fourth: bfloat16 [32, 32, 3, 3, 3], replicated, may hold values from -0.3125 to 0.3125
Outputs:
- features: bfloat16 [32, 8, 64, 2048], P(None, 'dev', 'gx', 'gy')
The draws below stay inside these ranges and needn't reach their ends.
All inputs are finite; a program needn't handle non-finite values.
Results may differ from the reference program's by a relative error of at most 0.0066.
Values may be sent and summed in bfloat16 or wider, within the bound.
No kernel may reach another device: no remote copies, remote signals or barrier semaphores. Data moves between devices by JAX's collectives and lax.ppermute only.
A program may use at most 64 MiB of HBM per device.

```python
import math
import jax
import jax.numpy as jnp
from jax import lax

C1 = 16
C2 = 32
SLAB = 16
NX = 128
NY = 4096


def shard_levels(key, dims, cuts, low, largest):
    level, own = 1.0, jax.random.fold_in(key, 6)
    for position, parts in cuts:
        draws = jnp.exp(jax.random.uniform(jax.random.fold_in(own, position), (parts,), jnp.float32, low / len(cuts), largest / len(cuts)))
        level = level * jnp.repeat(draws, dims[position] // parts).reshape([-1 if axis == position else 1 for axis in range(len(dims))])
    return level


def bell_draw(own_key, extent, scale, reach, shards=(), held_as=jnp.bfloat16):
    array = jax.random.normal(own_key, extent, jnp.float32) * scale
    if len(shards) > 0:
        array = shard_levels(own_key, extent, shards, -0.22, 0.18) * array
    return jnp.clip(array, min=-reach, max=reach).astype(held_as)


def setup_inputs(seed: int = 0) -> dict:
    keys = jax.random.split(jax.random.key(seed), 6)
    volume = bell_draw(keys[0], (C1, SLAB, NX, NY), 1.0, 6.0, ((2, 32), (3, 16)))
    w_first = bell_draw(keys[1], (C1, C1, 3, 3, 3), (27 * C1 // 2) ** -0.5, 0.4375)
    w_second = bell_draw(keys[2], (C1, C1, 3, 3, 3), (27 * C1 // 2) ** -0.5, 0.4375)
    w_third = bell_draw(keys[3], (C2, C1, 3, 3, 3), (27 * C1 // 2) ** -0.5, 0.4375)
    w_fourth = bell_draw(keys[4], (C2, C2, 3, 3, 3), (27 * C2 // 2) ** -0.5, 0.3125)
    return dict(volume=volume, w_first=w_first, w_second=w_second, w_third=w_third, w_fourth=w_fourth)


NUMBERS = ("NCDHW", "OIDHW", "NCDHW")


def conv_relu(source, weight):
    channels, depth_cells, row_cells, col_cells = source.shape
    padded = jnp.pad(source, ((0, 0), (1, 1), (1, 1), (1, 1)))
    block_rows = math.gcd(row_cells, 16)
    starts = jnp.arange(row_cells // block_rows, dtype=jnp.int32) * block_rows
    kernel = weight.astype(jnp.float32)

    def one_block(start):
        piece = lax.dynamic_slice_in_dim(padded, start, block_rows + 2, 2).astype(jnp.float32)
        output = lax.conv_general_dilated(piece[None], kernel, (1, 1, 1), "VALID", dimension_numbers=NUMBERS, precision=lax.Precision.HIGHEST)
        return jnp.maximum(output[0], 0.0).astype(jnp.bfloat16)

    blocks = lax.map(one_block, starts)
    out_chans = weight.shape[0]
    return jnp.moveaxis(blocks, 0, 2).reshape(out_chans, depth_cells, row_cells, col_cells)


def pool_pairs(source):
    channels, depth_cells, row_cells, col_cells = source.shape
    shaped = source.reshape(channels, depth_cells // 2, 2, row_cells // 2, 2, col_cells // 2, 2)
    return jnp.max(shaped, axis=(2, 4, 6))


def reference(volume, w_first, w_second, w_third, w_fourth):
    level_one = conv_relu(volume, w_first)
    level_two = conv_relu(level_one, w_second)
    pooled = pool_pairs(level_two)
    coarse = conv_relu(pooled, w_third)
    return conv_relu(coarse, w_fourth)
```

```python
import jax
import jax.numpy as jnp
from jax import lax
from jax.experimental import pallas as pl
from jax.experimental.pallas import tpu as pltpu
from jax.sharding import PartitionSpec as P

F32 = jnp.float32
BF16 = jnp.bfloat16
HALO = 16
COLS = 256
WIDE = COLS + 2 * HALO
HALF = WIDE // 2
VMEM_LIMIT = 48 * 1024 * 1024


def call(kernel, outs, scratch, flops, moved):
    return pl.pallas_call(
        kernel,
        out_shape=outs,
        scratch_shapes=scratch,
        compiler_params=pltpu.CompilerParams(vmem_limit_bytes=VMEM_LIMIT),
        cost_estimate=pl.CostEstimate(flops=flops, bytes_accessed=moved, transcendentals=0),
    )


def pack_kernel(x_ref, top, bottom, left, right, left_top, left_bottom, right_top, right_bottom, wide):
    wide[...] = x_ref[...].astype(F32)
    for r in range(4):
        image = wide[:, r, :].reshape(16, 16, COLS)
        image = jnp.transpose(image, (1, 0, 2)).reshape(256, COLS)
        image = jnp.transpose(image, (1, 0)).astype(BF16)
        first, last = image[:HALO], image[COLS - HALO :]
        left[r] = first
        right[r] = last
        half = r % 2
        if r < 2:
            top[half] = image
            left_top[half] = first
            right_top[half] = last
        else:
            bottom[half] = image
            left_bottom[half] = first
            right_bottom[half] = last


def one_hot(rows, lanes, of_lane):
    row = lax.broadcasted_iota(jnp.int32, (rows, lanes), 0)
    lane = lax.broadcasted_iota(jnp.int32, (rows, lanes), 1)
    return jnp.where(of_lane(lane) == row, 1.0, 0.0).astype(BF16)


def band(w_ref, out_ref, ins, outs, depths, lanes, o_of, z_of, tap_of):
    spread = jnp.dot(w_ref[...], one_hot(outs, lanes, o_of), preferred_element_type=F32)
    lane = lax.broadcasted_iota(jnp.int32, (ins, lanes), 1)
    z = z_of(lane)
    for zin in range(depths):
        tap = tap_of(zin, z)
        masks = [tap == a for a in range(3)]
        for b in range(3):
            for c in range(3):
                block = jnp.zeros((ins, lanes), F32)
                for a in range(3):
                    at = ((a * 3 + b) * 3 + c) * ins
                    block = jnp.where(masks[a], spread[at : at + ins], block)
                row = (b * depths + zin) * ins
                out_ref[row : row + ins, c * lanes : (c + 1) * lanes] = block.astype(BF16)


def weights_kernel(w1, w2, w3, w4, b1, b2, b3, b4):
    dev = lax.axis_index("dev")

    def same(zin, z):
        return zin - z + 1

    band(w1, b1, 16, 16, 16, 256, lambda n: n % 16, lambda n: n // 16, same)
    band(w2, b2, 16, 16, 16, 256, lambda n: n % 16, lambda n: 2 * ((n // 16) % 8) + n // 128, same)

    def shifted(zin, z):
        at = 2 * dev - 1 + z
        return jnp.where((at >= 0) & (at < 8), zin - at + 1, -1)

    band(w3, b3, 16, 32, 8, 128, lambda n: n % 32, lambda n: n // 32, shifted)
    band(w4, b4, 32, 32, 4, 128, lambda n: n // 2, lambda n: n % 2, lambda zin, z: zin - z)


def taps(rows, band_ref):
    lanes = rows[0].shape[1]
    lanes = band_ref.shape[1] // 3
    size = rows[0].shape[0]
    acc = jnp.dot(jnp.concatenate(rows, axis=1), band_ref[...], preferred_element_type=F32)
    total = pltpu.roll(acc[:, :lanes], 1, 0) + acc[:, lanes : 2 * lanes] + pltpu.roll(acc[:, 2 * lanes :], size - 1, 0)
    return jnp.maximum(total, 0.0)


def fine_kernel(top, bottom, up, down, left, right, up_left, up_right, down_left, down_right, b1, b2, pooled, x, level, wide):
    gx, dev, gy = lax.axis_index("gx"), lax.axis_index("dev"), lax.axis_index("gy")
    tile = gx * 4 + dev
    last_tile = 4 * lax.axis_size("gx") - 1
    last_gy = lax.axis_size("gy") - 1
    for r in range(2):
        for at, main, near, far in (
            (0, up[r], up_left[r], up_right[r]),
            (2, top[r], left[r], right[r]),
            (4, bottom[r], left[2 + r], right[2 + r]),
            (6, down[r], down_left[r], down_right[r]),
        ):
            x[at + r, :HALO] = near
            x[at + r, HALO : HALO + COLS] = main
            x[at + r, HALO + COLS :] = far
    for q in range(6):
        level[q] = taps([x[q], x[q + 1], x[q + 2]], b1).astype(BF16)

    @pl.when(gy == 0)
    def _():
        level[:, :HALO] = jnp.zeros((6, HALO, 256), BF16)

    @pl.when(gy == last_gy)
    def _():
        level[:, HALO + COLS :] = jnp.zeros((6, HALO, 256), BF16)

    @pl.when(tile == 0)
    def _():
        level[0] = jnp.zeros((WIDE, 256), BF16)

    @pl.when(tile == last_tile)
    def _():
        level[5] = jnp.zeros((WIDE, 256), BF16)

    col = lax.broadcasted_iota(jnp.int32, (HALF, 128), 0)
    inside = ((col >= HALO // 2) | (gy > 0)) & ((col < HALF - HALO // 2) | (gy < last_gy))
    for pair in range(2):
        two = [taps([level[q], level[q + 1], level[q + 2]], b2) for q in (2 * pair, 2 * pair + 1)]
        both = jnp.maximum(two[0], two[1])
        wide[...] = jnp.maximum(both[:, :128], both[:, 128:])
        most = jnp.maximum(wide[pl.ds(0, HALF, stride=2), :], wide[pl.ds(1, HALF, stride=2), :])
        pooled[pair] = jnp.where(inside, most, 0.0).astype(BF16)


def coarse_kernel(own, r1, r2, r3, q0, q1, q2, q3, b3, b4, out, x, level, wide):
    gx, dev, gy = lax.axis_index("gx"), lax.axis_index("dev"), lax.axis_index("gy")
    last_gx = lax.axis_size("gx") - 1
    last_gy = lax.axis_size("gy") - 1
    for k, part in enumerate((own, r1, r2, r3)):
        x[pl.ds(2 + 2 * ((dev + 4 - k) % 4), 2)] = part[...]
    for m, part in enumerate((q0, q1, q2, q3)):

        @pl.when(dev == m)
        def _():
            x[0:2] = part[...]

        @pl.when(dev == 3 - m)
        def _():
            x[10:12] = part[...]

    col = lax.broadcasted_iota(jnp.int32, (HALF, 128), 0)
    inside = ((col >= HALO // 2) | (gy > 0)) & ((col < HALF - HALO // 2) | (gy < last_gy))
    for q in range(10):
        keep = inside
        if q == 0:
            keep = keep & (gx > 0)
        if q == 9:
            keep = keep & (gx < last_gx)
        level[q] = jnp.where(keep, taps([x[q], x[q + 1], x[q + 2]], b3), 0.0).astype(BF16)
    for q in range(8):
        features = taps([level[q], level[q + 1], level[q + 2]], b4)
        turned = jnp.transpose(features[HALO // 2 : HALO // 2 + 128], (1, 0))
        wide[pl.ds(q, 64, stride=8), :] = turned[:64]
    out[...] = wide[...].astype(BF16)


def shift(cells, row_step, col_step):
    groups, col_tiles, devs = (lax.axis_size(axis) for axis in ("gx", "gy", "dev"))
    pairs = []
    for g in range(groups):
        for t in range(col_tiles):
            for d in range(devs):
                tile, col_tile = g * devs + d + row_step, t + col_step
                if 0 <= tile < groups * devs and 0 <= col_tile < col_tiles:
                    target = ((tile // devs) * col_tiles + col_tile) * devs + tile % devs
                    pairs.append(((g * col_tiles + t) * devs + d, target))
    return lax.ppermute(cells, ("gx", "gy", "dev"), pairs)


def body(volume, w_first, w_second, w_third, w_fourth):
    groups, devs = lax.axis_size("gx"), lax.axis_size("dev")
    sds = jax.ShapeDtypeStruct
    x = volume.reshape(256, 4, COLS)
    ends = sds((4, HALO, 256), BF16)
    corner = sds((2, HALO, 256), BF16)
    main = sds((2, COLS, 256), BF16)
    top, bottom, left, right, left_top, left_bottom, right_top, right_bottom = call(
        pack_kernel, [main, main, ends, ends, corner, corner, corner, corner], [pltpu.VMEM((256, 4, COLS), F32)], 0, 1 << 20
    )(x)

    rows = ("gx", "dev")
    up = shift(bottom, 1, 0)
    down = shift(top, -1, 0)
    from_left = shift(right, 0, 1)
    from_right = shift(left, 0, -1)
    up_left = shift(right_bottom, 1, 1)
    up_right = shift(left_bottom, 1, -1)
    down_left = shift(right_top, -1, 1)
    down_right = shift(left_top, -1, -1)

    def by_tap(weight):
        return jnp.transpose(weight, (2, 3, 4, 1, 0)).reshape(27 * weight.shape[1], weight.shape[0])

    b1, b2, b3, b4 = call(
        weights_kernel,
        [sds((768, 768), BF16), sds((768, 768), BF16), sds((384, 384), BF16), sds((384, 384), BF16)],
        [],
        0,
        3 << 20,
    )(by_tap(w_first), by_tap(w_second), by_tap(w_third), by_tap(w_fourth))

    pooled = call(
        fine_kernel,
        sds((2, HALF, 128), BF16),
        [pltpu.VMEM((8, WIDE, 256), BF16), pltpu.VMEM((6, WIDE, 256), BF16), pltpu.VMEM((WIDE, 128), F32)],
        2 * 10 * WIDE * 768 * 768,
        5 << 20,
    )(top, bottom, up, down, from_left, from_right, up_left, up_right, down_left, down_right, b1, b2)

    spread = [lax.ppermute(pooled, "dev", [(i, (i + k) % devs) for i in range(devs)]) for k in (1, 2, 3)]
    edge = []
    for m in range(4):
        pairs = [(g * devs + 3, (g + 1) * devs + m) for g in range(groups - 1)]
        pairs += [(g * devs, (g - 1) * devs + 3 - m) for g in range(1, groups)]
        edge.append(lax.ppermute(pooled, rows, pairs))

    out = call(
        coarse_kernel,
        sds((512, 128), BF16),
        [pltpu.VMEM((12, HALF, 128), BF16), pltpu.VMEM((10, HALF, 128), BF16), pltpu.VMEM((512, 128), F32)],
        2 * 18 * HALF * 384 * 384,
        2 << 20,
    )(pooled, *spread, *edge, b3, b4)
    return out.reshape(32, 2, 8, 128)


def solution(mesh):
    return jax.shard_map(
        body,
        mesh=mesh,
        in_specs=(P(None, None, ("gx", "dev"), "gy"), P(), P(), P(), P()),
        out_specs=P(None, "dev", "gx", "gy"),
        check_vma=False,
    )
```

```python
import jax
import jax.numpy as jnp
from jax import lax
from jax.experimental import pallas as pl
from jax.experimental.pallas import tpu as pltpu
from jax.sharding import PartitionSpec as P

F32 = jnp.float32
BF16 = jnp.bfloat16
HALO = 16
COLS = 256
WIDE = COLS + 2 * HALO
HALF = WIDE // 2
VMEM_LIMIT = 48 * 1024 * 1024


def call(kernel, outs, scratch, flops, moved):
    return pl.pallas_call(
        kernel,
        out_shape=outs,
        scratch_shapes=scratch,
        compiler_params=pltpu.CompilerParams(vmem_limit_bytes=VMEM_LIMIT),
        cost_estimate=pl.CostEstimate(flops=flops, bytes_accessed=moved, transcendentals=0),
    )


def pack_kernel(x_ref, top, bottom, left, right, wide):
    wide[...] = x_ref[...].astype(F32)
    for r in range(4):
        image = wide[:, r, :].reshape(16, 16, COLS)
        image = jnp.transpose(image, (1, 0, 2)).reshape(256, COLS)
        image = jnp.transpose(image, (1, 0)).astype(BF16)
        left[r] = image[:HALO]
        right[r] = image[COLS - HALO :]
        half = top if r < 2 else bottom
        half[r % 2] = image


def join_kernel(top, bottom, left, right, top_wide, bottom_wide):
    for at, main, wide in ((0, top, top_wide), (2, bottom, bottom_wide)):
        for r in range(2):
            wide[r, :HALO] = left[at + r]
            wide[r, HALO : HALO + COLS] = main[r]
            wide[r, HALO + COLS :] = right[at + r]


def one_hot(rows, lanes, of_lane):
    row = lax.broadcasted_iota(jnp.int32, (rows, lanes), 0)
    lane = lax.broadcasted_iota(jnp.int32, (rows, lanes), 1)
    return jnp.where(of_lane(lane) == row, 1.0, 0.0).astype(BF16)


def band(w_ref, out_ref, ins, outs, depths, lanes, o_of, z_of, tap_of):
    spread = jnp.dot(w_ref[...], one_hot(outs, lanes, o_of), preferred_element_type=F32)
    lane = lax.broadcasted_iota(jnp.int32, (ins, lanes), 1)
    z = z_of(lane)
    for zin in range(depths):
        tap = tap_of(zin, z)
        masks = [tap == a for a in range(3)]
        for b in range(3):
            for c in range(3):
                block = jnp.zeros((ins, lanes), F32)
                for a in range(3):
                    at = ((a * 3 + b) * 3 + c) * ins
                    block = jnp.where(masks[a], spread[at : at + ins], block)
                row = (b * depths + zin) * ins
                out_ref[row : row + ins, c * lanes : (c + 1) * lanes] = block.astype(BF16)


def weights_kernel(w1, w2, w3, w4, b1, b2, b3, b4):
    def same(zin, z):
        return zin - z + 1

    band(w1, b1, 16, 16, 16, 256, lambda n: n % 16, lambda n: n // 16, same)
    band(w2, b2, 16, 16, 16, 256, lambda n: n % 16, lambda n: 2 * ((n // 16) % 8) + n // 128, same)

    band(w3, b3, 16, 32, 8, 256, lambda n: n % 32, lambda n: n // 32, same)
    band(w4, b4, 32, 32, 8, 256, lambda n: (n % 64) // 2, lambda n: 2 * (n // 64) + n % 2, same)


def taps(rows, band_ref):
    lanes = band_ref.shape[1] // 3
    size = rows[0].shape[0]
    acc = jnp.dot(jnp.concatenate(rows, axis=1), band_ref[...], preferred_element_type=F32)
    total = pltpu.roll(acc[:, :lanes], 1, 0) + acc[:, lanes : 2 * lanes] + pltpu.roll(acc[:, 2 * lanes :], size - 1, 0)
    return jnp.maximum(total, 0.0)


def place():
    tile = lax.axis_index("gx") * lax.axis_size("dev") + lax.axis_index("dev")
    gy = lax.axis_index("gy")
    last_tile = lax.axis_size("gx") * lax.axis_size("dev") - 1
    return tile, last_tile, gy, lax.axis_size("gy") - 1


def fine_kernel(top, bottom, up, down, b1, b2, pooled, level, wide):
    tile, last_tile, gy, last_gy = place()
    x = [part[r] for part in (up, top, bottom, down) for r in range(2)]
    for q in range(6):
        level[q] = taps([x[q], x[q + 1], x[q + 2]], b1).astype(BF16)

    @pl.when(gy == 0)
    def _():
        level[:, :HALO] = jnp.zeros((6, HALO, 256), BF16)

    @pl.when(gy == last_gy)
    def _():
        level[:, HALO + COLS :] = jnp.zeros((6, HALO, 256), BF16)

    @pl.when(tile == 0)
    def _():
        level[0] = jnp.zeros((WIDE, 256), BF16)

    @pl.when(tile == last_tile)
    def _():
        level[5] = jnp.zeros((WIDE, 256), BF16)

    col = lax.broadcasted_iota(jnp.int32, (HALF, 128), 0)
    inside = ((col >= HALO // 2) | (gy > 0)) & ((col < HALF - HALO // 2) | (gy < last_gy))
    for pair in range(2):
        two = [taps([level[q], level[q + 1], level[q + 2]], b2) for q in (2 * pair, 2 * pair + 1)]
        both = jnp.maximum(two[0], two[1])
        wide[...] = jnp.maximum(both[:, :128], both[:, 128:])
        most = jnp.maximum(wide[pl.ds(0, HALF, stride=2), :], wide[pl.ds(1, HALF, stride=2), :])
        pooled[pair] = jnp.where(inside, most, 0.0).astype(BF16)


def coarse_kernel(own, up, down, b3, b4, kept, to_1, to_2, to_3, level, parts):
    tile, last_tile, gy, last_gy = place()
    dev = lax.axis_index("dev")
    x = [part[r] for part in (up, own, down) for r in range(2)]
    col = lax.broadcasted_iota(jnp.int32, (HALF, 256), 0)
    inside = ((col >= HALO // 2) | (gy > 0)) & ((col < HALF - HALO // 2) | (gy < last_gy))
    for q in range(4):
        keep = inside
        if q == 0:
            keep = keep & (tile > 0)
        if q == 3:
            keep = keep & (tile < last_tile)
        level[q] = jnp.where(keep, taps([x[q], x[q + 1], x[q + 2]], b3), 0.0).astype(BF16)
    for q in range(2):
        features = taps([level[q], level[q + 1], level[q + 2]], b4)
        turned = jnp.transpose(features[HALO // 2 : HALO // 2 + 128], (1, 0))
        for part in range(4):
            parts[part, q] = turned[part * 64 : (part + 1) * 64].astype(BF16)
    for k, to in enumerate((kept, to_1, to_2, to_3)):
        to[...] = parts[(dev + k) % 4]


def last_kernel(kept, from_1, from_2, from_3, out, rows, wide):
    dev = lax.axis_index("dev")
    for k, part in enumerate((kept, from_1, from_2, from_3)):
        rows[pl.ds(2 * ((dev + 4 - k) % 4), 2)] = part[...].astype(F32)
    for r in range(8):
        wide[pl.ds(r, 64, stride=8), :] = rows[r]
    out[...] = wide[...].astype(BF16)


def shift(cells, row_step, col_step):
    groups, col_tiles, devs = (lax.axis_size(axis) for axis in ("gx", "gy", "dev"))
    pairs = []
    for g in range(groups):
        for t in range(col_tiles):
            for d in range(devs):
                tile, col_tile = g * devs + d + row_step, t + col_step
                if 0 <= tile < groups * devs and 0 <= col_tile < col_tiles:
                    target = ((tile // devs) * col_tiles + col_tile) * devs + tile % devs
                    pairs.append(((g * col_tiles + t) * devs + d, target))
    return lax.ppermute(cells, ("gx", "gy", "dev"), pairs)


def by_tap(weight):
    return jnp.transpose(weight, (2, 3, 4, 1, 0)).reshape(27 * weight.shape[1], weight.shape[0])


def body(volume, w_first, w_second, w_third, w_fourth):
    devs = lax.axis_size("dev")
    sds = jax.ShapeDtypeStruct
    main = sds((2, COLS, 256), BF16)
    ends = sds((4, HALO, 256), BF16)
    both = sds((2, WIDE, 256), BF16)
    top, bottom, left, right = call(
        pack_kernel, [main, main, ends, ends], [pltpu.VMEM((256, 4, COLS), F32)], 0, 1 << 20
    )(volume.reshape(256, 4, COLS))
    from_left = shift(right, 0, 1)
    from_right = shift(left, 0, -1)
    top, bottom = call(join_kernel, [both, both], [], 0, 1 << 20)(top, bottom, from_left, from_right)
    up = shift(bottom, 1, 0)
    down = shift(top, -1, 0)

    b1, b2, b3, b4 = call(
        weights_kernel,
        [sds((768, 768), BF16), sds((768, 768), BF16), sds((384, 768), BF16), sds((768, 768), BF16)],
        [],
        0,
        4 << 20,
    )(by_tap(w_first), by_tap(w_second), by_tap(w_third), by_tap(w_fourth))

    pooled = call(
        fine_kernel,
        sds((2, HALF, 128), BF16),
        [pltpu.VMEM((6, WIDE, 256), BF16), pltpu.VMEM((WIDE, 128), F32)],
        2 * 10 * WIDE * 768 * 768,
        5 << 20,
    )(top, bottom, up, down, b1, b2)
    up = shift(pooled, 1, 0)
    down = shift(pooled, -1, 0)

    part = sds((2, 64, 128), BF16)
    kept, *sent = call(
        coarse_kernel,
        [part, part, part, part],
        [pltpu.VMEM((4, HALF, 256), BF16), pltpu.VMEM((4, 2, 64, 128), BF16)],
        2 * 4 * HALF * 768 * 768,
        2 << 20,
    )(pooled, up, down, b3, b4)
    received = [lax.ppermute(cells, "dev", [(i, (i + k + 1) % devs) for i in range(devs)]) for k, cells in enumerate(sent)]
    out = call(
        last_kernel, sds((512, 128), BF16), [pltpu.VMEM((8, 64, 128), F32), pltpu.VMEM((512, 128), F32)], 0, 1 << 18
    )(kept, *received)
    return out.reshape(32, 2, 8, 128)


def solution(mesh):
    return jax.shard_map(
        body,
        mesh=mesh,
        in_specs=(P(None, None, ("gx", "dev"), "gy"), P(), P(), P(), P()),
        out_specs=P(None, "dev", "gx", "gy"),
        check_vma=False,
    )
```

```python
import jax
import jax.numpy as jnp
from jax import lax
from jax.experimental import pallas as pl
from jax.experimental.pallas import tpu as pltpu
from jax.sharding import PartitionSpec as P

F32 = jnp.float32
BF16 = jnp.bfloat16
HALO = 16
COLS = 256
WIDE = COLS + 2 * HALO
HALF = WIDE // 2
VMEM_LIMIT = 48 * 1024 * 1024


def call(kernel, outs, scratch, flops, moved):
    return pl.pallas_call(
        kernel,
        out_shape=outs,
        scratch_shapes=scratch,
        compiler_params=pltpu.CompilerParams(vmem_limit_bytes=VMEM_LIMIT),
        cost_estimate=pl.CostEstimate(flops=flops, bytes_accessed=moved, transcendentals=0),
    )


def pack_kernel(x_ref, top, bottom, left, right, wide):
    wide[...] = x_ref[...].astype(F32)
    for r in range(4):
        image = wide[:, r, :].reshape(16, 16, COLS)
        image = jnp.transpose(image, (1, 0, 2)).reshape(256, COLS)
        image = jnp.transpose(image, (1, 0)).astype(BF16)
        left[r] = image[:HALO]
        right[r] = image[COLS - HALO :]
        half = top if r < 2 else bottom
        half[r % 2] = image


def join_kernel(top, bottom, left, right, top_wide, bottom_wide):
    for at, main, wide in ((0, top, top_wide), (2, bottom, bottom_wide)):
        for r in range(2):
            wide[r, :HALO] = left[at + r]
            wide[r, HALO : HALO + COLS] = main[r]
            wide[r, HALO + COLS :] = right[at + r]


def one_hot(rows, lanes, of_lane):
    row = lax.broadcasted_iota(jnp.int32, (rows, lanes), 0)
    lane = lax.broadcasted_iota(jnp.int32, (rows, lanes), 1)
    return jnp.where(of_lane(lane) == row, 1.0, 0.0).astype(BF16)


def band(w_ref, out_ref, ins, outs, depths, lanes, o_of, z_of, tap_of):
    spread = jnp.dot(w_ref[...], one_hot(outs, lanes, o_of), preferred_element_type=F32)
    lane = lax.broadcasted_iota(jnp.int32, (ins, lanes), 1)
    z = z_of(lane)
    for zin in range(depths):
        tap = tap_of(zin, z)
        masks = [tap == a for a in range(3)]
        for b in range(3):
            for c in range(3):
                block = jnp.zeros((ins, lanes), F32)
                for a in range(3):
                    at = ((a * 3 + b) * 3 + c) * ins
                    block = jnp.where(masks[a], spread[at : at + ins], block)
                row = (b * depths + zin) * ins
                out_ref[row : row + ins, c * lanes : (c + 1) * lanes] = block.astype(BF16)


def weights_kernel(w1, w2, w3, w4, b1, b2, b3, b4):
    def same(zin, z):
        return zin - z + 1

    band(w1, b1, 16, 16, 16, 256, lambda n: n % 16, lambda n: n // 16, same)
    band(w2, b2, 16, 16, 16, 256, lambda n: n % 16, lambda n: 2 * ((n // 16) % 8) + n // 128, same)

    band(w3, b3, 16, 32, 8, 256, lambda n: n % 32, lambda n: n // 32, same)
    band(w4, b4, 32, 32, 8, 256, lambda n: (n % 64) // 2, lambda n: 2 * (n // 64) + n % 2, same)


def taps(rows, band_ref):
    lanes = band_ref.shape[1] // 3
    size = rows[0].shape[0]
    acc = jnp.dot(jnp.concatenate(rows, axis=1), band_ref[...], preferred_element_type=F32)
    total = pltpu.roll(acc[:, :lanes], 1, 0) + acc[:, lanes : 2 * lanes] + pltpu.roll(acc[:, 2 * lanes :], size - 1, 0)
    return jnp.maximum(total, 0.0)


def place():
    tile = lax.axis_index("gx") * lax.axis_size("dev") + lax.axis_index("dev")
    gy = lax.axis_index("gy")
    last_tile = lax.axis_size("gx") * lax.axis_size("dev") - 1
    return tile, last_tile, gy, lax.axis_size("gy") - 1


def fine_kernel(top, bottom, up, down, b1, b2, pooled, level, wide):
    tile, last_tile, gy, last_gy = place()
    x = [part[r] for part in (up, top, bottom, down) for r in range(2)]
    for q in range(6):
        level[q] = taps([x[q], x[q + 1], x[q + 2]], b1).astype(BF16)

    @pl.when(gy == 0)
    def _():
        level[:, :HALO] = jnp.zeros((6, HALO, 256), BF16)

    @pl.when(gy == last_gy)
    def _():
        level[:, HALO + COLS :] = jnp.zeros((6, HALO, 256), BF16)

    @pl.when(tile == 0)
    def _():
        level[0] = jnp.zeros((WIDE, 256), BF16)

    @pl.when(tile == last_tile)
    def _():
        level[5] = jnp.zeros((WIDE, 256), BF16)

    col = lax.broadcasted_iota(jnp.int32, (HALF, 128), 0)
    inside = ((col >= HALO // 2) | (gy > 0)) & ((col < HALF - HALO // 2) | (gy < last_gy))
    for pair in range(2):
        two = [taps([level[q], level[q + 1], level[q + 2]], b2) for q in (2 * pair, 2 * pair + 1)]
        both = jnp.maximum(two[0], two[1])
        wide[...] = jnp.maximum(both[:, :128], both[:, 128:])
        most = jnp.maximum(wide[pl.ds(0, HALF, stride=2), :], wide[pl.ds(1, HALF, stride=2), :])
        pooled[pair] = jnp.where(inside, most, 0.0).astype(BF16)


def coarse_kernel(own, up, down, b3, b4, parts, level):
    tile, last_tile, gy, last_gy = place()
    x = [part[r] for part in (up, own, down) for r in range(2)]
    col = lax.broadcasted_iota(jnp.int32, (HALF, 256), 0)
    inside = ((col >= HALO // 2) | (gy > 0)) & ((col < HALF - HALO // 2) | (gy < last_gy))
    for q in range(4):
        keep = inside
        if q == 0:
            keep = keep & (tile > 0)
        if q == 3:
            keep = keep & (tile < last_tile)
        level[q] = jnp.where(keep, taps([x[q], x[q + 1], x[q + 2]], b3), 0.0).astype(BF16)
    for q in range(2):
        features = taps([level[q], level[q + 1], level[q + 2]], b4)
        turned = jnp.transpose(features[HALO // 2 : HALO // 2 + 128], (1, 0))
        for part in range(4):
            parts[part, q] = turned[part * 64 : (part + 1) * 64].astype(BF16)


def last_kernel(parts, out, wide):
    for r in range(8):
        wide[pl.ds(r, 64, stride=8), :] = parts[r // 2, r % 2].astype(F32)
    out[...] = wide[...].astype(BF16)


def shift(cells, row_step, col_step):
    groups, col_tiles, devs = (lax.axis_size(axis) for axis in ("gx", "gy", "dev"))
    pairs = []
    for g in range(groups):
        for t in range(col_tiles):
            for d in range(devs):
                tile, col_tile = g * devs + d + row_step, t + col_step
                if 0 <= tile < groups * devs and 0 <= col_tile < col_tiles:
                    target = ((tile // devs) * col_tiles + col_tile) * devs + tile % devs
                    pairs.append(((g * col_tiles + t) * devs + d, target))
    return lax.ppermute(cells, ("gx", "gy", "dev"), pairs)


def by_tap(weight):
    return jnp.transpose(weight, (2, 3, 4, 1, 0)).reshape(27 * weight.shape[1], weight.shape[0])


def body(volume, w_first, w_second, w_third, w_fourth):
    sds = jax.ShapeDtypeStruct
    main = sds((2, COLS, 256), BF16)
    ends = sds((4, HALO, 256), BF16)
    both = sds((2, WIDE, 256), BF16)
    top, bottom, left, right = call(
        pack_kernel, [main, main, ends, ends], [pltpu.VMEM((256, 4, COLS), F32)], 0, 1 << 20
    )(volume.reshape(256, 4, COLS))
    from_left = shift(right, 0, 1)
    from_right = shift(left, 0, -1)
    top, bottom = call(join_kernel, [both, both], [], 0, 1 << 20)(top, bottom, from_left, from_right)
    up = shift(bottom, 1, 0)
    down = shift(top, -1, 0)

    b1, b2, b3, b4 = call(
        weights_kernel,
        [sds((768, 768), BF16), sds((768, 768), BF16), sds((384, 768), BF16), sds((768, 768), BF16)],
        [],
        0,
        4 << 20,
    )(by_tap(w_first), by_tap(w_second), by_tap(w_third), by_tap(w_fourth))

    pooled = call(
        fine_kernel,
        sds((2, HALF, 128), BF16),
        [pltpu.VMEM((6, WIDE, 256), BF16), pltpu.VMEM((WIDE, 128), F32)],
        2 * 10 * WIDE * 768 * 768,
        5 << 20,
    )(top, bottom, up, down, b1, b2)
    up = shift(pooled, 1, 0)
    down = shift(pooled, -1, 0)

    parts = call(
        coarse_kernel, sds((4, 2, 64, 128), BF16), [pltpu.VMEM((4, HALF, 256), BF16)], 2 * 4 * HALF * 768 * 768, 2 << 20
    )(pooled, up, down, b3, b4)
    parts = lax.all_to_all(parts, "dev", split_axis=0, concat_axis=0, tiled=True)
    out = call(last_kernel, sds((512, 128), BF16), [pltpu.VMEM((512, 128), F32)], 0, 1 << 18)(parts)
    return out.reshape(32, 2, 8, 128)


def solution(mesh):
    return jax.shard_map(
        body,
        mesh=mesh,
        in_specs=(P(None, None, ("gx", "dev"), "gy"), P(), P(), P(), P()),
        out_specs=P(None, "dev", "gx", "gy"),
        check_vma=False,
    )
```

```python
import jax
import jax.numpy as jnp
from jax import lax
from jax.experimental import pallas as pl
from jax.experimental.pallas import tpu as pltpu
from jax.sharding import PartitionSpec as P

F32 = jnp.float32
BF16 = jnp.bfloat16
HALO = 16
COLS = 256
WIDE = COLS + 2 * HALO
HALF = WIDE // 2
VMEM_LIMIT = 48 * 1024 * 1024


def call(kernel, outs, scratch, flops, moved):
    return pl.pallas_call(
        kernel,
        out_shape=outs,
        scratch_shapes=scratch,
        compiler_params=pltpu.CompilerParams(vmem_limit_bytes=VMEM_LIMIT),
        cost_estimate=pl.CostEstimate(flops=flops, bytes_accessed=moved, transcendentals=0),
    )


def pack_kernel(x_ref, top, bottom, wide):
    wide[...] = x_ref[...].astype(F32)
    for r in range(4):
        image = wide[:, r, :].reshape(16, 16, COLS)
        image = jnp.transpose(image, (1, 0, 2)).reshape(256, COLS)
        half = top if r < 2 else bottom
        half[r % 2] = jnp.transpose(image, (1, 0)).astype(BF16)


def ends_kernel(up, top, bottom, down, left, right):
    for at, part in enumerate((up, top, bottom, down)):
        for r in range(2):
            left[2 * at + r] = part[r, :HALO]
            right[2 * at + r] = part[r, COLS - HALO :]


def one_hot(rows, lanes, of_lane):
    row = lax.broadcasted_iota(jnp.int32, (rows, lanes), 0)
    lane = lax.broadcasted_iota(jnp.int32, (rows, lanes), 1)
    return jnp.where(of_lane(lane) == row, 1.0, 0.0).astype(BF16)


def band(w_ref, out_ref, ins, outs, depths, lanes, o_of, z_of, tap_of):
    spread = jnp.dot(w_ref[...], one_hot(outs, lanes, o_of), preferred_element_type=F32)
    lane = lax.broadcasted_iota(jnp.int32, (ins, lanes), 1)
    z = z_of(lane)
    for zin in range(depths):
        tap = tap_of(zin, z)
        masks = [tap == a for a in range(3)]
        for b in range(3):
            for c in range(3):
                block = jnp.zeros((ins, lanes), F32)
                for a in range(3):
                    at = ((a * 3 + b) * 3 + c) * ins
                    block = jnp.where(masks[a], spread[at : at + ins], block)
                row = (b * depths + zin) * ins
                out_ref[row : row + ins, c * lanes : (c + 1) * lanes] = block.astype(BF16)


def weights_kernel(w1, w2, w3, w4, b1, b2, b3, b4):
    def same(zin, z):
        return zin - z + 1

    band(w1, b1, 16, 16, 16, 256, lambda n: n % 16, lambda n: n // 16, same)
    band(w2, b2, 16, 16, 16, 256, lambda n: n % 16, lambda n: 2 * ((n // 16) % 8) + n // 128, same)

    band(w3, b3, 16, 32, 8, 256, lambda n: n % 32, lambda n: n // 32, same)
    band(w4, b4, 32, 32, 8, 256, lambda n: (n % 64) // 2, lambda n: 2 * (n // 64) + n % 2, same)


def taps(rows, band_ref):
    lanes = band_ref.shape[1] // 3
    size = rows[0].shape[0]
    acc = jnp.dot(jnp.concatenate(rows, axis=1), band_ref[...], preferred_element_type=F32)
    total = pltpu.roll(acc[:, :lanes], 1, 0) + acc[:, lanes : 2 * lanes] + pltpu.roll(acc[:, 2 * lanes :], size - 1, 0)
    return jnp.maximum(total, 0.0)


def place():
    tile = lax.axis_index("gx") * lax.axis_size("dev") + lax.axis_index("dev")
    gy = lax.axis_index("gy")
    last_tile = lax.axis_size("gx") * lax.axis_size("dev") - 1
    return tile, last_tile, gy, lax.axis_size("gy") - 1


def fine_kernel(up, top, bottom, down, left, right, b1, b2, pooled, x, level, wide):
    tile, last_tile, gy, last_gy = place()
    for at, part in enumerate((up, top, bottom, down)):
        for r in range(2):
            x[2 * at + r, :HALO] = left[2 * at + r]
            x[2 * at + r, HALO : HALO + COLS] = part[r]
            x[2 * at + r, HALO + COLS :] = right[2 * at + r]
    for q in range(6):
        level[q] = taps([x[q], x[q + 1], x[q + 2]], b1).astype(BF16)

    @pl.when(gy == 0)
    def _():
        level[:, :HALO] = jnp.zeros((6, HALO, 256), BF16)

    @pl.when(gy == last_gy)
    def _():
        level[:, HALO + COLS :] = jnp.zeros((6, HALO, 256), BF16)

    @pl.when(tile == 0)
    def _():
        level[0] = jnp.zeros((WIDE, 256), BF16)

    @pl.when(tile == last_tile)
    def _():
        level[5] = jnp.zeros((WIDE, 256), BF16)

    col = lax.broadcasted_iota(jnp.int32, (HALF, 128), 0)
    inside = ((col >= HALO // 2) | (gy > 0)) & ((col < HALF - HALO // 2) | (gy < last_gy))
    for pair in range(2):
        two = [taps([level[q], level[q + 1], level[q + 2]], b2) for q in (2 * pair, 2 * pair + 1)]
        both = jnp.maximum(two[0], two[1])
        wide[...] = jnp.maximum(both[:, :128], both[:, 128:])
        most = jnp.maximum(wide[pl.ds(0, HALF, stride=2), :], wide[pl.ds(1, HALF, stride=2), :])
        pooled[pair] = jnp.where(inside, most, 0.0).astype(BF16)


def coarse_kernel(own, up, down, b3, b4, parts, level):
    tile, last_tile, gy, last_gy = place()
    x = [part[r] for part in (up, own, down) for r in range(2)]
    col = lax.broadcasted_iota(jnp.int32, (HALF, 256), 0)
    inside = ((col >= HALO // 2) | (gy > 0)) & ((col < HALF - HALO // 2) | (gy < last_gy))
    for q in range(4):
        keep = inside
        if q == 0:
            keep = keep & (tile > 0)
        if q == 3:
            keep = keep & (tile < last_tile)
        level[q] = jnp.where(keep, taps([x[q], x[q + 1], x[q + 2]], b3), 0.0).astype(BF16)
    for q in range(2):
        features = taps([level[q], level[q + 1], level[q + 2]], b4)
        turned = jnp.transpose(features[HALO // 2 : HALO // 2 + 128], (1, 0))
        for part in range(4):
            parts[part, q] = turned[part * 64 : (part + 1) * 64].astype(BF16)


def last_kernel(parts, out, wide):
    for r in range(8):
        wide[pl.ds(r, 64, stride=8), :] = parts[r // 2, r % 2].astype(F32)
    out[...] = wide[...].astype(BF16)


def shift(cells, row_step, col_step):
    groups, col_tiles, devs = (lax.axis_size(axis) for axis in ("gx", "gy", "dev"))
    pairs = []
    for g in range(groups):
        for t in range(col_tiles):
            for d in range(devs):
                tile, col_tile = g * devs + d + row_step, t + col_step
                if 0 <= tile < groups * devs and 0 <= col_tile < col_tiles:
                    target = ((tile // devs) * col_tiles + col_tile) * devs + tile % devs
                    pairs.append(((g * col_tiles + t) * devs + d, target))
    return lax.ppermute(cells, ("gx", "gy", "dev"), pairs)


def by_tap(weight):
    return jnp.transpose(weight, (2, 3, 4, 1, 0)).reshape(27 * weight.shape[1], weight.shape[0])


def body(volume, w_first, w_second, w_third, w_fourth):
    sds = jax.ShapeDtypeStruct
    main = sds((2, COLS, 256), BF16)
    ends = sds((8, HALO, 256), BF16)
    top, bottom = call(pack_kernel, [main, main], [pltpu.VMEM((256, 4, COLS), F32)], 0, 1 << 20)(volume.reshape(256, 4, COLS))
    up = shift(bottom, 1, 0)
    down = shift(top, -1, 0)
    left, right = call(ends_kernel, [ends, ends], [], 0, 1 << 18)(up, top, bottom, down)
    from_left = shift(right, 0, 1)
    from_right = shift(left, 0, -1)

    b1, b2, b3, b4 = call(
        weights_kernel,
        [sds((768, 768), BF16), sds((768, 768), BF16), sds((384, 768), BF16), sds((768, 768), BF16)],
        [],
        0,
        4 << 20,
    )(by_tap(w_first), by_tap(w_second), by_tap(w_third), by_tap(w_fourth))

    pooled = call(
        fine_kernel,
        sds((2, HALF, 128), BF16),
        [pltpu.VMEM((8, WIDE, 256), BF16), pltpu.VMEM((6, WIDE, 256), BF16), pltpu.VMEM((WIDE, 128), F32)],
        2 * 10 * WIDE * 768 * 768,
        5 << 20,
    )(up, top, bottom, down, from_left, from_right, b1, b2)
    up = shift(pooled, 1, 0)
    down = shift(pooled, -1, 0)

    parts = call(
        coarse_kernel, sds((4, 2, 64, 128), BF16), [pltpu.VMEM((4, HALF, 256), BF16)], 2 * 4 * HALF * 768 * 768, 2 << 20
    )(pooled, up, down, b3, b4)
    parts = lax.all_to_all(parts, "dev", split_axis=0, concat_axis=0, tiled=True)
    out = call(last_kernel, sds((512, 128), BF16), [pltpu.VMEM((512, 128), F32)], 0, 1 << 18)(parts)
    return out.reshape(32, 2, 8, 128)


def solution(mesh):
    return jax.shard_map(
        body,
        mesh=mesh,
        in_specs=(P(None, None, ("gx", "dev"), "gy"), P(), P(), P(), P()),
        out_specs=P(None, "dev", "gx", "gy"),
        check_vma=False,
    )
```

```python
import jax
import jax.numpy as jnp
from jax import lax
from jax.experimental import pallas as pl
from jax.experimental.pallas import tpu as pltpu
from jax.sharding import PartitionSpec as P

F32 = jnp.float32
BF16 = jnp.bfloat16
HALO = 16
COLS = 256
WIDE = COLS + 2 * HALO
HALF = WIDE // 2
VMEM_LIMIT = 48 * 1024 * 1024


def call(kernel, outs, scratch, flops, moved):
    return pl.pallas_call(
        kernel,
        out_shape=outs,
        scratch_shapes=scratch,
        compiler_params=pltpu.CompilerParams(vmem_limit_bytes=VMEM_LIMIT),
        cost_estimate=pl.CostEstimate(flops=flops, bytes_accessed=moved, transcendentals=0),
    )


def pack_kernel(x_ref, to_a, to_b, wide, images):
    wide[...] = x_ref[...].astype(F32)
    for r in range(4):
        image = wide[:, r, :].reshape(16, 16, COLS)
        image = jnp.transpose(image, (1, 0, 2)).reshape(256, COLS)
        images[r] = jnp.transpose(image, (1, 0)).astype(BF16)
    odd = lax.axis_index("dev") % 2
    to_a[...] = images[pl.ds(2 - 2 * odd, 2)]
    to_b[...] = images[pl.ds(2 * odd, 2)]


def row_parts(from_a, from_b, to_a, to_b):
    odd = lax.axis_index("dev") % 2
    return ((6 - 6 * odd, from_a), (6 * odd, from_b), (4 - 2 * odd, to_a), (2 + 2 * odd, to_b))


def ends_kernel(from_b, from_a, to_a, to_b, after, to_c, to_d, ends):
    for at, part in row_parts(from_a, from_b, to_a, to_b):
        for r in range(2):
            ends[0, at + r] = part[r, :HALO]
            ends[1, at + r] = part[r, COLS - HALO :]
    odd = lax.axis_index("gy") % 2
    to_c[...] = ends[1 - odd]
    to_d[...] = ends[odd]


def one_hot(rows, lanes, of_lane):
    row = lax.broadcasted_iota(jnp.int32, (rows, lanes), 0)
    lane = lax.broadcasted_iota(jnp.int32, (rows, lanes), 1)
    return jnp.where(of_lane(lane) == row, 1.0, 0.0).astype(BF16)


def band(w_ref, out_ref, ins, outs, depths, lanes, o_of, z_of, tap_of):
    spread = jnp.dot(w_ref[...], one_hot(outs, lanes, o_of), preferred_element_type=F32)
    lane = lax.broadcasted_iota(jnp.int32, (ins, lanes), 1)
    z = z_of(lane)
    for zin in range(depths):
        tap = tap_of(zin, z)
        masks = [tap == a for a in range(3)]
        for b in range(3):
            for c in range(3):
                block = jnp.zeros((ins, lanes), F32)
                for a in range(3):
                    at = ((a * 3 + b) * 3 + c) * ins
                    block = jnp.where(masks[a], spread[at : at + ins], block)
                row = (b * depths + zin) * ins
                out_ref[row : row + ins, c * lanes : (c + 1) * lanes] = block.astype(BF16)


def weights_kernel(w1, w2, w3, w4, b1, b2, b3, b4):
    def same(zin, z):
        return zin - z + 1

    band(w1, b1, 16, 16, 16, 256, lambda n: n % 16, lambda n: n // 16, same)
    band(w2, b2, 16, 16, 16, 256, lambda n: n % 16, lambda n: 2 * ((n // 16) % 8) + n // 128, same)

    band(w3, b3, 16, 32, 8, 256, lambda n: n % 32, lambda n: n // 32, same)
    band(w4, b4, 32, 32, 8, 256, lambda n: (n % 64) // 2, lambda n: 2 * (n // 64) + n % 2, same)


def taps(rows, band_ref):
    lanes = band_ref.shape[1] // 3
    size = rows[0].shape[0]
    acc = jnp.dot(jnp.concatenate(rows, axis=1), band_ref[...], preferred_element_type=F32)
    total = pltpu.roll(acc[:, :lanes], 1, 0) + acc[:, lanes : 2 * lanes] + pltpu.roll(acc[:, 2 * lanes :], size - 1, 0)
    return jnp.maximum(total, 0.0)


def place():
    tile = lax.axis_index("gx") * lax.axis_size("dev") + lax.axis_index("dev")
    gy = lax.axis_index("gy")
    last_tile = lax.axis_size("gx") * lax.axis_size("dev") - 1
    return tile, last_tile, gy, lax.axis_size("gy") - 1


def halved(cells, wide):
    size = cells.shape[0]
    wide[0:size, :] = jnp.maximum(cells[:, :128], cells[:, 128:])
    return jnp.maximum(wide[pl.ds(0, size // 2, stride=2), :], wide[pl.ds(1, size // 2, stride=2), :])


def centre_kernel(from_b, from_a, to_a, to_b, b1, b2, pooled, x, level, wide):
    tile, last_tile, gy, last_gy = place()
    for at, part in row_parts(from_a, from_b, to_a, to_b):
        x[pl.ds(at, 2)] = part[...]
    for q in range(6):
        level[q] = taps([x[q], x[q + 1], x[q + 2]], b1).astype(BF16)

    @pl.when(tile == 0)
    def _():
        level[0] = jnp.zeros((COLS, 256), BF16)

    @pl.when(tile == last_tile)
    def _():
        level[5] = jnp.zeros((COLS, 256), BF16)

    for pair in range(2):
        two = [taps([level[q], level[q + 1], level[q + 2]], b2) for q in (2 * pair, 2 * pair + 1)]
        pooled[pair] = halved(jnp.maximum(two[0], two[1]), wide)


def strips_kernel(from_d, from_c, to_c, to_d, centre, b1, b2, pooled, x, level, wide):
    tile, last_tile, gy, last_gy = place()
    odd = gy % 2
    x[3 - 3 * odd] = from_c[...]
    x[3 * odd] = from_d[...]
    x[2 - odd] = to_c[...]
    x[1 + odd] = to_d[...]
    rows = jnp.concatenate([x[part, r] for r in range(8) for part in range(4)], axis=0)
    level[...] = taps([rows[0:384], rows[64:448], rows[128:512]], b1).astype(BF16)
    for q in range(6):

        @pl.when(gy == 0)
        def _():
            level[64 * q : 64 * q + 16] = jnp.zeros((16, 256), BF16)

        @pl.when(gy == last_gy)
        def _():
            level[64 * q + 48 : 64 * q + 64] = jnp.zeros((16, 256), BF16)

    @pl.when(tile == 0)
    def _():
        level[0:64] = jnp.zeros((64, 256), BF16)

    @pl.when(tile == last_tile)
    def _():
        level[320:384] = jnp.zeros((64, 256), BF16)

    two = taps([level[0:256], level[64:320], level[128:384]], b2)
    col = lax.broadcasted_iota(jnp.int32, (32, 128), 0)
    inside = ((col >= 8) | (gy > 0)) & ((col < 24) | (gy < last_gy))
    outer = lax.broadcasted_iota(jnp.int32, (8, 128), 0) < 4
    for pair in range(2):
        at = 128 * pair
        strip = halved(jnp.maximum(two[at : at + 64], two[at + 64 : at + 128]), wide)
        strip = jnp.where(inside, strip, 0.0)
        main = centre[pair]
        low = jnp.where(outer, strip[8:16], main[0:8])
        high = jnp.where(outer, main[120:128], strip[16:24])
        pooled[pair] = jnp.concatenate([strip[0:8], low, main[8:120], high, strip[24:32]], axis=0).astype(BF16)


def coarse_kernel(own, from_b, from_a, b3, b4, parts, x, level):
    tile, last_tile, gy, last_gy = place()
    odd = lax.axis_index("dev") % 2
    x[2:4] = own[...]
    x[pl.ds(4 - 4 * odd, 2)] = from_a[...]
    x[pl.ds(4 * odd, 2)] = from_b[...]
    col = lax.broadcasted_iota(jnp.int32, (HALF, 256), 0)
    inside = ((col >= HALO // 2) | (gy > 0)) & ((col < HALF - HALO // 2) | (gy < last_gy))
    for q in range(4):
        keep = inside
        if q == 0:
            keep = keep & (tile > 0)
        if q == 3:
            keep = keep & (tile < last_tile)
        level[q] = jnp.where(keep, taps([x[q], x[q + 1], x[q + 2]], b3), 0.0).astype(BF16)
    for q in range(2):
        features = taps([level[q], level[q + 1], level[q + 2]], b4)
        turned = jnp.transpose(features[HALO // 2 : HALO // 2 + 128], (1, 0))
        for part in range(4):
            parts[part, q] = turned[part * 64 : (part + 1) * 64].astype(BF16)


def last_kernel(parts, out, wide):
    for r in range(8):
        wide[pl.ds(r, 64, stride=8), :] = parts[r // 2, r % 2].astype(F32)
    out[...] = wide[...].astype(BF16)


def swap_rows(cells, first):
    groups, col_tiles, devs = (lax.axis_size(axis) for axis in ("gx", "gy", "dev"))
    pairs = []
    for low in range(first, groups * devs - 1, 2):
        for t in range(col_tiles):
            one, two = (((tile // devs) * col_tiles + t) * devs + tile % devs for tile in (low, low + 1))
            pairs += [(one, two), (two, one)]
    return lax.ppermute(cells, ("gx", "gy", "dev"), pairs)


def swap_cols(cells, first):
    pairs = []
    for low in range(first, lax.axis_size("gy") - 1, 2):
        pairs += [(low, low + 1), (low + 1, low)]
    return lax.ppermute(cells, "gy", pairs)


def by_tap(weight):
    return jnp.transpose(weight, (2, 3, 4, 1, 0)).reshape(27 * weight.shape[1], weight.shape[0])


def body(volume, w_first, w_second, w_third, w_fourth):
    sds = jax.ShapeDtypeStruct
    main = sds((2, COLS, 256), BF16)
    ends = sds((8, HALO, 256), BF16)
    to_a, to_b = call(
        pack_kernel, [main, main], [pltpu.VMEM((256, 4, COLS), F32), pltpu.VMEM((4, COLS, 256), BF16)], 0, 1 << 20
    )(volume.reshape(256, 4, COLS))
    from_b = swap_rows(to_b, 1)
    from_a = swap_rows(to_a, 0)

    b1, b2, b3, b4 = call(
        weights_kernel,
        [sds((768, 768), BF16), sds((768, 768), BF16), sds((384, 768), BF16), sds((768, 768), BF16)],
        [],
        0,
        4 << 20,
    )(by_tap(w_first), by_tap(w_second), by_tap(w_third), by_tap(w_fourth))

    to_c, to_d = call(ends_kernel, [ends, ends], [pltpu.VMEM((2, 8, HALO, 256), BF16)], 0, 1 << 18)(
        from_b, from_a, to_a, to_b, b3
    )
    from_d = swap_cols(to_d, 1)
    from_c = swap_cols(to_c, 0)
    centre = call(
        centre_kernel,
        sds((2, 128, 128), F32),
        [pltpu.VMEM((8, COLS, 256), BF16), pltpu.VMEM((6, COLS, 256), BF16), pltpu.VMEM((COLS, 128), F32)],
        2 * 10 * COLS * 768 * 768,
        5 << 20,
    )(from_b, from_a, to_a, to_b, b1, b2)
    pooled = call(
        strips_kernel,
        sds((2, HALF, 128), BF16),
        [pltpu.VMEM((4, 8, HALO, 256), BF16), pltpu.VMEM((384, 256), BF16), pltpu.VMEM((64, 128), F32)],
        2 * 640 * 768 * 768,
        4 << 20,
    )(from_d, from_c, to_c, to_d, centre, b1, b2)
    from_b = swap_rows(pooled, 1)
    from_a = swap_rows(pooled, 0)

    parts = call(
        coarse_kernel, sds((4, 2, 64, 128), BF16), [pltpu.VMEM((6, HALF, 128), BF16), pltpu.VMEM((4, HALF, 256), BF16)], 2 * 4 * HALF * 768 * 768, 2 << 20
    )(pooled, from_b, from_a, b3, b4)
    parts = lax.all_to_all(parts, "dev", split_axis=0, concat_axis=0, tiled=True)
    out = call(last_kernel, sds((512, 128), BF16), [pltpu.VMEM((512, 128), F32)], 0, 1 << 18)(parts)
    return out.reshape(32, 2, 8, 128)


def solution(mesh):
    return jax.shard_map(
        body,
        mesh=mesh,
        in_specs=(P(None, None, ("gx", "dev"), "gy"), P(), P(), P(), P()),
        out_specs=P(None, "dev", "gx", "gy"),
        check_vma=False,
    )
```

```python
import jax
import jax.numpy as jnp
from jax import lax
from jax.experimental import pallas as pl
from jax.experimental.pallas import tpu as pltpu
from jax.sharding import PartitionSpec as P

F32 = jnp.float32
BF16 = jnp.bfloat16
HALO = 16
COLS = 256
WIDE = COLS + 2 * HALO
HALF = WIDE // 2
VMEM_LIMIT = 48 * 1024 * 1024


def call(kernel, outs, scratch, flops, moved):
    return pl.pallas_call(
        kernel,
        out_shape=outs,
        scratch_shapes=scratch,
        compiler_params=pltpu.CompilerParams(vmem_limit_bytes=VMEM_LIMIT),
        cost_estimate=pl.CostEstimate(flops=flops, bytes_accessed=moved, transcendentals=0),
    )


def pack_kernel(x_ref, to_a, to_b, wide, images):
    wide[...] = x_ref[...].astype(F32)
    for r in range(4):
        image = wide[:, r, :].reshape(16, 16, COLS)
        image = jnp.transpose(image, (1, 0, 2)).reshape(256, COLS)
        images[r] = jnp.transpose(image, (1, 0)).astype(BF16)
    odd = lax.axis_index("dev") % 2
    to_a[...] = images[pl.ds(2 - 2 * odd, 2)]
    to_b[...] = images[pl.ds(2 * odd, 2)]


def row_parts(from_a, from_b, to_a, to_b):
    odd = lax.axis_index("dev") % 2
    return ((6 - 6 * odd, from_a), (6 * odd, from_b), (4 - 2 * odd, to_a), (2 + 2 * odd, to_b))


def ends_kernel(from_b, from_a, to_a, to_b, after, to_c, to_d, ends):
    for at, part in row_parts(from_a, from_b, to_a, to_b):
        low = [part[r, :16].astype(F32)[:8] for r in range(2)]
        high = [part[r, COLS - 16 :].astype(F32)[8:] for r in range(2)]
        ends[0, at // 2] = jnp.concatenate(low, axis=0).astype(BF16)
        ends[1, at // 2] = jnp.concatenate(high, axis=0).astype(BF16)
    odd = lax.axis_index("gy") % 2
    to_c[...] = ends[1 - odd]
    to_d[...] = ends[odd]


def one_hot(rows, lanes, of_lane):
    row = lax.broadcasted_iota(jnp.int32, (rows, lanes), 0)
    lane = lax.broadcasted_iota(jnp.int32, (rows, lanes), 1)
    return jnp.where(of_lane(lane) == row, 1.0, 0.0).astype(BF16)


def band(w_ref, out_ref, ins, outs, depths, lanes, o_of, z_of, tap_of):
    spread = jnp.dot(w_ref[...], one_hot(outs, lanes, o_of), preferred_element_type=F32)
    lane = lax.broadcasted_iota(jnp.int32, (ins, lanes), 1)
    z = z_of(lane)
    for zin in range(depths):
        tap = tap_of(zin, z)
        masks = [tap == a for a in range(3)]
        for b in range(3):
            for c in range(3):
                block = jnp.zeros((ins, lanes), F32)
                for a in range(3):
                    at = ((a * 3 + b) * 3 + c) * ins
                    block = jnp.where(masks[a], spread[at : at + ins], block)
                row = (b * depths + zin) * ins
                out_ref[row : row + ins, c * lanes : (c + 1) * lanes] = block.astype(BF16)


def weights_kernel(w1, w2, w3, w4, b1, b2, b3, b4):
    def same(zin, z):
        return zin - z + 1

    band(w1, b1, 16, 16, 16, 256, lambda n: n % 16, lambda n: n // 16, same)
    band(w2, b2, 16, 16, 16, 256, lambda n: n % 16, lambda n: 2 * ((n // 16) % 8) + n // 128, same)

    band(w3, b3, 16, 32, 8, 256, lambda n: n % 32, lambda n: n // 32, same)
    band(w4, b4, 32, 32, 8, 256, lambda n: (n % 64) // 2, lambda n: 2 * (n // 64) + n % 2, same)


def taps(rows, band_ref):
    lanes = band_ref.shape[1] // 3
    size = rows[0].shape[0]
    acc = jnp.dot(jnp.concatenate(rows, axis=1), band_ref[...], preferred_element_type=F32)
    total = pltpu.roll(acc[:, :lanes], 1, 0) + acc[:, lanes : 2 * lanes] + pltpu.roll(acc[:, 2 * lanes :], size - 1, 0)
    return jnp.maximum(total, 0.0)


def place():
    tile = lax.axis_index("gx") * lax.axis_size("dev") + lax.axis_index("dev")
    gy = lax.axis_index("gy")
    last_tile = lax.axis_size("gx") * lax.axis_size("dev") - 1
    return tile, last_tile, gy, lax.axis_size("gy") - 1


def halved(cells, wide):
    size = cells.shape[0]
    wide[0:size, :] = jnp.maximum(cells[:, :128], cells[:, 128:])
    return jnp.maximum(wide[pl.ds(0, size // 2, stride=2), :], wide[pl.ds(1, size // 2, stride=2), :])


def centre_kernel(from_b, from_a, to_a, to_b, b1, b2, pooled, x, level, wide):
    tile, last_tile, gy, last_gy = place()
    for at, part in row_parts(from_a, from_b, to_a, to_b):
        x[pl.ds(at, 2)] = part[...]
    for q in range(6):
        level[q] = taps([x[q], x[q + 1], x[q + 2]], b1).astype(BF16)

    @pl.when(tile == 0)
    def _():
        level[0] = jnp.zeros((COLS, 256), BF16)

    @pl.when(tile == last_tile)
    def _():
        level[5] = jnp.zeros((COLS, 256), BF16)

    for pair in range(2):
        two = [taps([level[q], level[q + 1], level[q + 2]], b2) for q in (2 * pair, 2 * pair + 1)]
        pooled[pair] = halved(jnp.maximum(two[0], two[1]), wide)


def strips_kernel(from_d, from_c, to_c, to_d, centre, b1, b2, pooled, x, wide):
    tile, last_tile, gy, last_gy = place()
    odd = gy % 2
    x[3 - 3 * odd] = from_c[...]
    x[3 * odd] = from_d[...]
    x[2 - odd] = to_c[...]
    x[1 + odd] = to_d[...]
    pieces = []
    for two in range(4):
        parts = [x[part, two].astype(F32) for part in range(4)]
        pieces += [part[8 * r : 8 * r + 8] for r in range(2) for part in parts]
    rows = jnp.concatenate(pieces, axis=0).astype(BF16)
    level = taps([rows[0:192], rows[32:224], rows[64:256]], b1)
    at = lax.broadcasted_iota(jnp.int32, (192, 256), 0)
    col = at % 32
    keep = ((col >= 8) | (gy > 0)) & ((col < 24) | (gy < last_gy))
    keep = keep & ((at >= 32) | (tile > 0)) & ((at < 160) | (tile < last_tile))
    level = jnp.where(keep, level, 0.0).astype(BF16)
    two = taps([level[0:128], level[32:160], level[64:192]], b2)
    row = lax.broadcasted_iota(jnp.int32, (8, 128), 0)
    for pair in range(2):
        at = 64 * pair
        strip = halved(jnp.maximum(two[at : at + 32], two[at + 32 : at + 64]), wide)
        low, high = pltpu.roll(strip[0:8], 4, 0), pltpu.roll(strip[8:16], 4, 0)
        main = centre[pair]
        parts = [
            jnp.where(gy > 0, low, 0.0),
            jnp.where(row < 2, low, main[0:8]),
            main[8:120],
            jnp.where(row < 6, main[120:128], high),
            jnp.where(gy < last_gy, high, 0.0),
        ]
        pooled[pair] = jnp.concatenate(parts, axis=0).astype(BF16)


def coarse_kernel(own, from_b, from_a, b3, b4, parts, x, level):
    tile, last_tile, gy, last_gy = place()
    odd = lax.axis_index("dev") % 2
    x[2:4] = own[...]
    x[pl.ds(4 - 4 * odd, 2)] = from_a[...]
    x[pl.ds(4 * odd, 2)] = from_b[...]
    col = lax.broadcasted_iota(jnp.int32, (HALF, 256), 0)
    inside = ((col >= HALO // 2) | (gy > 0)) & ((col < HALF - HALO // 2) | (gy < last_gy))
    for q in range(4):
        keep = inside
        if q == 0:
            keep = keep & (tile > 0)
        if q == 3:
            keep = keep & (tile < last_tile)
        level[q] = jnp.where(keep, taps([x[q], x[q + 1], x[q + 2]], b3), 0.0).astype(BF16)
    for q in range(2):
        features = taps([level[q], level[q + 1], level[q + 2]], b4)
        turned = jnp.transpose(features[HALO // 2 : HALO // 2 + 128], (1, 0))
        for part in range(4):
            parts[part, q] = turned[part * 64 : (part + 1) * 64].astype(BF16)


def last_kernel(parts, out, wide):
    for r in range(8):
        wide[pl.ds(r, 64, stride=8), :] = parts[r // 2, r % 2].astype(F32)
    out[...] = wide[...].astype(BF16)


def swap_rows(cells, first):
    groups, col_tiles, devs = (lax.axis_size(axis) for axis in ("gx", "gy", "dev"))
    pairs = []
    for low in range(first, groups * devs - 1, 2):
        for t in range(col_tiles):
            one, two = (((tile // devs) * col_tiles + t) * devs + tile % devs for tile in (low, low + 1))
            pairs += [(one, two), (two, one)]
    return lax.ppermute(cells, ("gx", "gy", "dev"), pairs)


def swap_cols(cells, first):
    pairs = []
    for low in range(first, lax.axis_size("gy") - 1, 2):
        pairs += [(low, low + 1), (low + 1, low)]
    return lax.ppermute(cells, "gy", pairs)


def by_tap(weight):
    return jnp.transpose(weight, (2, 3, 4, 1, 0)).reshape(27 * weight.shape[1], weight.shape[0])


def body(volume, w_first, w_second, w_third, w_fourth):
    sds = jax.ShapeDtypeStruct
    main = sds((2, COLS, 256), BF16)
    ends = sds((4, 16, 256), BF16)
    to_a, to_b = call(
        pack_kernel, [main, main], [pltpu.VMEM((256, 4, COLS), F32), pltpu.VMEM((4, COLS, 256), BF16)], 0, 1 << 20
    )(volume.reshape(256, 4, COLS))
    from_b = swap_rows(to_b, 1)
    from_a = swap_rows(to_a, 0)

    b1, b2, b3, b4 = call(
        weights_kernel,
        [sds((768, 768), BF16), sds((768, 768), BF16), sds((384, 768), BF16), sds((768, 768), BF16)],
        [],
        0,
        4 << 20,
    )(by_tap(w_first), by_tap(w_second), by_tap(w_third), by_tap(w_fourth))

    to_c, to_d = call(ends_kernel, [ends, ends], [pltpu.VMEM((2, 4, 16, 256), BF16)], 0, 1 << 18)(
        from_b, from_a, to_a, to_b, b3
    )
    from_d = swap_cols(to_d, 1)
    from_c = swap_cols(to_c, 0)
    centre = call(
        centre_kernel,
        sds((2, 128, 128), F32),
        [pltpu.VMEM((8, COLS, 256), BF16), pltpu.VMEM((6, COLS, 256), BF16), pltpu.VMEM((COLS, 128), F32)],
        2 * 10 * COLS * 768 * 768,
        5 << 20,
    )(from_b, from_a, to_a, to_b, b1, b2)
    pooled = call(
        strips_kernel,
        sds((2, HALF, 128), BF16),
        [pltpu.VMEM((4, 4, 16, 256), BF16), pltpu.VMEM((32, 128), F32)],
        2 * 320 * 768 * 768,
        4 << 20,
    )(from_d, from_c, to_c, to_d, centre, b1, b2)
    from_b = swap_rows(pooled, 1)
    from_a = swap_rows(pooled, 0)

    parts = call(
        coarse_kernel, sds((4, 2, 64, 128), BF16), [pltpu.VMEM((6, HALF, 128), BF16), pltpu.VMEM((4, HALF, 256), BF16)], 2 * 4 * HALF * 768 * 768, 2 << 20
    )(pooled, from_b, from_a, b3, b4)
    parts = lax.all_to_all(parts, "dev", split_axis=0, concat_axis=0, tiled=True)
    out = call(last_kernel, sds((512, 128), BF16), [pltpu.VMEM((512, 128), F32)], 0, 1 << 18)(parts)
    return out.reshape(32, 2, 8, 128)


def solution(mesh):
    return jax.shard_map(
        body,
        mesh=mesh,
        in_specs=(P(None, None, ("gx", "dev"), "gy"), P(), P(), P(), P()),
        out_specs=P(None, "dev", "gx", "gy"),
        check_vma=False,
    )
```

```python
import jax
import jax.numpy as jnp
from jax import lax
from jax.experimental import pallas as pl
from jax.experimental.pallas import tpu as pltpu
from jax.sharding import PartitionSpec as P

F32 = jnp.float32
BF16 = jnp.bfloat16
HALO = 16
COLS = 256
WIDE = COLS + 2 * HALO
HALF = WIDE // 2
VMEM_LIMIT = 48 * 1024 * 1024


def call(kernel, outs, scratch, flops, moved):
    return pl.pallas_call(
        kernel,
        out_shape=outs,
        scratch_shapes=scratch,
        compiler_params=pltpu.CompilerParams(vmem_limit_bytes=VMEM_LIMIT),
        cost_estimate=pl.CostEstimate(flops=flops, bytes_accessed=moved, transcendentals=0),
    )


def pack_kernel(x_ref, to_a, to_b, wide, images):
    wide[...] = x_ref[...].astype(F32)
    for r in range(4):
        image = wide[:, r, :].reshape(16, 16, COLS)
        image = jnp.transpose(image, (1, 0, 2)).reshape(256, COLS)
        images[r] = jnp.transpose(image, (1, 0)).astype(BF16)
    odd = lax.axis_index("dev") % 2
    to_a[...] = images[pl.ds(2 - 2 * odd, 2)]
    to_b[...] = images[pl.ds(2 * odd, 2)]


def row_parts(from_a, from_b, to_a, to_b):
    odd = lax.axis_index("dev") % 2
    return ((6 - 6 * odd, from_a), (6 * odd, from_b), (4 - 2 * odd, to_a), (2 + 2 * odd, to_b))


def ends_kernel(from_b, from_a, to_a, to_b, after, to_c, to_d, ends):
    for at, part in row_parts(from_a, from_b, to_a, to_b):
        low = [part[r, :16].astype(F32)[:8] for r in range(2)]
        high = [part[r, COLS - 16 :].astype(F32)[8:] for r in range(2)]
        ends[0, at // 2] = jnp.concatenate(low, axis=0).astype(BF16)
        ends[1, at // 2] = jnp.concatenate(high, axis=0).astype(BF16)
    odd = lax.axis_index("gy") % 2
    to_c[...] = ends[1 - odd]
    to_d[...] = ends[odd]


def one_hot(rows, lanes, of_lane):
    row = lax.broadcasted_iota(jnp.int32, (rows, lanes), 0)
    lane = lax.broadcasted_iota(jnp.int32, (rows, lanes), 1)
    return jnp.where(of_lane(lane) == row, 1.0, 0.0).astype(BF16)


def band(w_ref, out_ref, ins, outs, depths, lanes, o_of, z_of, tap_of):
    spread = jnp.dot(w_ref[...], one_hot(outs, lanes, o_of), preferred_element_type=F32)
    lane = lax.broadcasted_iota(jnp.int32, (ins, lanes), 1)
    z = z_of(lane)
    for zin in range(depths):
        tap = tap_of(zin, z)
        masks = [tap == a for a in range(3)]
        for b in range(3):
            for c in range(3):
                block = jnp.zeros((ins, lanes), F32)
                for a in range(3):
                    at = ((a * 3 + b) * 3 + c) * ins
                    block = jnp.where(masks[a], spread[at : at + ins], block)
                row = (b * depths + zin) * ins
                out_ref[row : row + ins, c * lanes : (c + 1) * lanes] = block.astype(BF16)


def weights_kernel(w1, w2, w3, w4, b1, b2, b3, b4):
    def same(zin, z):
        return zin - z + 1

    band(w1, b1, 16, 16, 16, 256, lambda n: n % 16, lambda n: n // 16, same)
    band(w2, b2, 16, 16, 16, 256, lambda n: n % 16, lambda n: 2 * ((n // 16) % 8) + n // 128, same)

    dev = lax.axis_index("dev")

    def near(zin, z):
        at = 2 * dev - 1 + z
        return jnp.where((at >= 0) & (at < 8), zin - at + 1, -1)

    band(w3, b3, 16, 32, 8, 128, lambda n: n % 32, lambda n: n // 32, near)
    band(w4, b4, 32, 32, 4, 128, lambda n: n // 2, lambda n: n % 2, lambda zin, z: zin - z)


def taps(rows, band_ref):
    lanes = band_ref.shape[1] // 3
    size = rows[0].shape[0]
    acc = jnp.dot(jnp.concatenate(rows, axis=1), band_ref[...], preferred_element_type=F32)
    total = pltpu.roll(acc[:, :lanes], 1, 0) + acc[:, lanes : 2 * lanes] + pltpu.roll(acc[:, 2 * lanes :], size - 1, 0)
    return jnp.maximum(total, 0.0)


def place():
    tile = lax.axis_index("gx") * lax.axis_size("dev") + lax.axis_index("dev")
    gy = lax.axis_index("gy")
    last_tile = lax.axis_size("gx") * lax.axis_size("dev") - 1
    return tile, last_tile, gy, lax.axis_size("gy") - 1


def halved(cells, wide):
    size = cells.shape[0]
    wide[0:size, :] = jnp.maximum(cells[:, :128], cells[:, 128:])
    return jnp.maximum(wide[pl.ds(0, size // 2, stride=2), :], wide[pl.ds(1, size // 2, stride=2), :])


def centre_kernel(from_b, from_a, to_a, to_b, b1, b2, pooled, x, level, wide):
    tile, last_tile, gy, last_gy = place()
    for at, part in row_parts(from_a, from_b, to_a, to_b):
        x[pl.ds(at, 2)] = part[...]
    for q in range(6):
        level[q] = taps([x[q], x[q + 1], x[q + 2]], b1).astype(BF16)

    @pl.when(tile == 0)
    def _():
        level[0] = jnp.zeros((COLS, 256), BF16)

    @pl.when(tile == last_tile)
    def _():
        level[5] = jnp.zeros((COLS, 256), BF16)

    for pair in range(2):
        two = [taps([level[q], level[q + 1], level[q + 2]], b2) for q in (2 * pair, 2 * pair + 1)]
        pooled[pair] = halved(jnp.maximum(two[0], two[1]), wide)


def strips_kernel(from_d, from_c, to_c, to_d, centre, b1, b2, pooled, x, wide):
    tile, last_tile, gy, last_gy = place()
    odd = gy % 2
    x[3 - 3 * odd] = from_c[...]
    x[3 * odd] = from_d[...]
    x[2 - odd] = to_c[...]
    x[1 + odd] = to_d[...]
    pieces = []
    for two in range(4):
        parts = [x[part, two].astype(F32) for part in range(4)]
        pieces += [part[8 * r : 8 * r + 8] for r in range(2) for part in parts]
    rows = jnp.concatenate(pieces, axis=0).astype(BF16)
    level = taps([rows[0:192], rows[32:224], rows[64:256]], b1)
    at = lax.broadcasted_iota(jnp.int32, (192, 256), 0)
    col = at % 32
    keep = ((col >= 8) | (gy > 0)) & ((col < 24) | (gy < last_gy))
    keep = keep & ((at >= 32) | (tile > 0)) & ((at < 160) | (tile < last_tile))
    level = jnp.where(keep, level, 0.0).astype(BF16)
    two = taps([level[0:128], level[32:160], level[64:192]], b2)
    row = lax.broadcasted_iota(jnp.int32, (8, 128), 0)
    for pair in range(2):
        at = 64 * pair
        strip = halved(jnp.maximum(two[at : at + 32], two[at + 32 : at + 64]), wide)
        low, high = pltpu.roll(strip[0:8], 4, 0), pltpu.roll(strip[8:16], 4, 0)
        main = centre[pair]
        parts = [
            jnp.where(gy > 0, low, 0.0),
            jnp.where(row < 2, low, main[0:8]),
            main[8:120],
            jnp.where(row < 6, main[120:128], high),
            jnp.where(gy < last_gy, high, 0.0),
        ]
        done = jnp.concatenate(parts, axis=0).astype(BF16)
        for copy in range(4):
            pooled[copy, pair] = done


def edges_kernel(group, to_a, to_b):
    odd = lax.axis_index("gx") % 2
    to_a[...] = group[3 - 3 * odd]
    to_b[...] = group[3 * odd]


def coarse_row(rows, b3, keep):
    gy, last_gy = lax.axis_index("gy"), lax.axis_size("gy") - 1
    col = lax.broadcasted_iota(jnp.int32, (HALF, 128), 0)
    inside = ((col >= HALO // 2) | (gy > 0)) & ((col < HALF - HALO // 2) | (gy < last_gy)) & keep
    return jnp.where(inside, taps(rows, b3), 0.0).astype(BF16)


def feature_row(rows, b4):
    features = taps(rows, b4)
    return jnp.transpose(features[HALO // 2 : HALO // 2 + 128], (1, 0))[:64]


def inner_kernel(group, b3, b4, level, turned):
    x = [group[part, r] for part in range(4) for r in range(2)]
    for q in range(6):
        level[q] = coarse_row([x[q], x[q + 1], x[q + 2]], b3, True)
    for q in range(4):
        turned[q] = feature_row([level[q], level[q + 1], level[q + 2]], b4)


def outer_kernel(from_b, from_a, group, inner, turned, b3, b4, out, x, level, wide):
    gx = lax.axis_index("gx")
    odd = gx % 2
    x[pl.ds(2 - 2 * odd, 2)] = from_a[...]
    x[pl.ds(2 * odd, 2)] = from_b[...]
    above = [x[0], x[1], group[0, 0], group[0, 1]]
    below = [group[3, 0], group[3, 1], x[2], x[3]]
    for q in range(2):
        level[q] = coarse_row(above[q : q + 3], b3, (gx > 0) | (q > 0))
        level[2 + q] = coarse_row(below[q : q + 3], b3, (gx < lax.axis_size("gx") - 1) | (q < 1))
    above = [level[0], level[1], inner[0], inner[1]]
    below = [inner[4], inner[5], level[2], level[3]]
    for q in range(2):
        wide[pl.ds(q, 64, stride=8), :] = feature_row(above[q : q + 3], b4)
        wide[pl.ds(6 + q, 64, stride=8), :] = feature_row(below[q : q + 3], b4)
    for q in range(4):
        wide[pl.ds(2 + q, 64, stride=8), :] = turned[q]
    out[...] = wide[...].astype(BF16)


def swap_rows(cells, first):
    groups, col_tiles, devs = (lax.axis_size(axis) for axis in ("gx", "gy", "dev"))
    pairs = []
    for low in range(first, groups * devs - 1, 2):
        for t in range(col_tiles):
            one, two = (((tile // devs) * col_tiles + t) * devs + tile % devs for tile in (low, low + 1))
            pairs += [(one, two), (two, one)]
    return lax.ppermute(cells, ("gx", "gy", "dev"), pairs)


def swap(cells, axis, first):
    pairs = []
    for low in range(first, lax.axis_size(axis) - 1, 2):
        pairs += [(low, low + 1), (low + 1, low)]
    return lax.ppermute(cells, axis, pairs)


def by_tap(weight):
    return jnp.transpose(weight, (2, 3, 4, 1, 0)).reshape(27 * weight.shape[1], weight.shape[0])


def body(volume, w_first, w_second, w_third, w_fourth):
    sds = jax.ShapeDtypeStruct
    main = sds((2, COLS, 256), BF16)
    ends = sds((4, 16, 256), BF16)
    to_a, to_b = call(
        pack_kernel, [main, main], [pltpu.VMEM((256, 4, COLS), F32), pltpu.VMEM((4, COLS, 256), BF16)], 0, 1 << 20
    )(volume.reshape(256, 4, COLS))
    from_b = swap_rows(to_b, 1)
    from_a = swap_rows(to_a, 0)

    b1, b2, b3, b4 = call(
        weights_kernel,
        [sds((768, 768), BF16), sds((768, 768), BF16), sds((384, 384), BF16), sds((384, 384), BF16)],
        [],
        0,
        4 << 20,
    )(by_tap(w_first), by_tap(w_second), by_tap(w_third), by_tap(w_fourth))

    to_c, to_d = call(ends_kernel, [ends, ends], [pltpu.VMEM((2, 4, 16, 256), BF16)], 0, 1 << 18)(
        from_b, from_a, to_a, to_b, b3
    )
    from_d = swap(to_d, "gy", 1)
    from_c = swap(to_c, "gy", 0)
    centre = call(
        centre_kernel,
        sds((2, 128, 128), F32),
        [pltpu.VMEM((8, COLS, 256), BF16), pltpu.VMEM((6, COLS, 256), BF16), pltpu.VMEM((COLS, 128), F32)],
        2 * 10 * COLS * 768 * 768,
        5 << 20,
    )(from_b, from_a, to_a, to_b, b1, b2)
    group = call(
        strips_kernel,
        sds((4, 2, HALF, 128), BF16),
        [pltpu.VMEM((4, 4, 16, 256), BF16), pltpu.VMEM((32, 128), F32)],
        2 * 320 * 768 * 768,
        4 << 20,
    )(from_d, from_c, to_c, to_d, centre, b1, b2)
    group = lax.all_to_all(group, "dev", split_axis=0, concat_axis=0, tiled=True)
    edge = sds((2, HALF, 128), BF16)
    to_a, to_b = call(edges_kernel, [edge, edge], [], 0, 1 << 18)(group)
    from_b = swap(to_b, "gx", 1)
    from_a = swap(to_a, "gx", 0)
    inner, turned = call(
        inner_kernel, [sds((6, HALF, 128), BF16), sds((4, 64, 128), F32)], [], 2 * 10 * HALF * 384 * 384, 1 << 20
    )(group, b3, b4)
    out = call(
        outer_kernel,
        sds((512, 128), BF16),
        [pltpu.VMEM((4, HALF, 128), BF16), pltpu.VMEM((4, HALF, 128), BF16), pltpu.VMEM((512, 128), F32)],
        2 * 8 * HALF * 384 * 384,
        1 << 20,
    )(from_b, from_a, group, inner, turned, b3, b4)
    return out.reshape(32, 2, 8, 128)


def solution(mesh):
    return jax.shard_map(
        body,
        mesh=mesh,
        in_specs=(P(None, None, ("gx", "dev"), "gy"), P(), P(), P(), P()),
        out_specs=P(None, "dev", "gx", "gy"),
        check_vma=False,
    )
```

```python
import jax
import jax.numpy as jnp
from jax import lax
from jax.experimental import pallas as pl
from jax.experimental.pallas import tpu as pltpu
from jax.sharding import PartitionSpec as P

F32 = jnp.float32
BF16 = jnp.bfloat16
HALO = 16
COLS = 256
WIDE = COLS + 2 * HALO
HALF = WIDE // 2
VMEM_LIMIT = 48 * 1024 * 1024


def call(kernel, outs, scratch, flops, moved):
    return pl.pallas_call(
        kernel,
        out_shape=outs,
        scratch_shapes=scratch,
        compiler_params=pltpu.CompilerParams(vmem_limit_bytes=VMEM_LIMIT),
        cost_estimate=pl.CostEstimate(flops=flops, bytes_accessed=moved, transcendentals=0),
    )


def pack_kernel(x_ref, to_a, to_b, wide, images):
    wide[...] = x_ref[...].astype(F32)
    for r in range(4):
        image = wide[:, r, :].reshape(16, 16, COLS)
        image = jnp.transpose(image, (1, 0, 2)).reshape(256, COLS)
        images[r] = jnp.transpose(image, (1, 0)).astype(BF16)
    odd = lax.axis_index("dev") % 2
    to_a[...] = images[pl.ds(2 - 2 * odd, 2)]
    to_b[...] = images[pl.ds(2 * odd, 2)]


def row_parts(from_a, from_b, to_a, to_b):
    odd = lax.axis_index("dev") % 2
    return ((6 - 6 * odd, from_a), (6 * odd, from_b), (4 - 2 * odd, to_a), (2 + 2 * odd, to_b))


def ends_kernel(from_b, from_a, to_a, to_b, after, to_c, to_d, ends):
    for at, part in row_parts(from_a, from_b, to_a, to_b):
        low = [part[r, :16].astype(F32)[:8] for r in range(2)]
        high = [part[r, COLS - 16 :].astype(F32)[8:] for r in range(2)]
        ends[0, at // 2] = jnp.concatenate(low, axis=0).astype(BF16)
        ends[1, at // 2] = jnp.concatenate(high, axis=0).astype(BF16)
    odd = lax.axis_index("gy") % 2
    to_c[...] = ends[1 - odd]
    to_d[...] = ends[odd]


def one_hot(rows, lanes, of_lane):
    row = lax.broadcasted_iota(jnp.int32, (rows, lanes), 0)
    lane = lax.broadcasted_iota(jnp.int32, (rows, lanes), 1)
    return jnp.where(of_lane(lane) == row, 1.0, 0.0).astype(BF16)


def band(w_ref, out_ref, ins, outs, depths, lanes, o_of, z_of, tap_of):
    spread = jnp.dot(w_ref[...], one_hot(outs, lanes, o_of), preferred_element_type=F32)
    lane = lax.broadcasted_iota(jnp.int32, (ins, lanes), 1)
    z = z_of(lane)
    for zin in range(depths):
        tap = tap_of(zin, z)
        masks = [tap == a for a in range(3)]
        for b in range(3):
            for c in range(3):
                block = jnp.zeros((ins, lanes), F32)
                for a in range(3):
                    at = ((a * 3 + b) * 3 + c) * ins
                    block = jnp.where(masks[a], spread[at : at + ins], block)
                row = (b * depths + zin) * ins
                out_ref[row : row + ins, c * lanes : (c + 1) * lanes] = block.astype(BF16)


def weights_kernel(w1, w2, w3, w4, b1, b2, b3, b4):
    def same(zin, z):
        return zin - z + 1

    band(w1, b1, 16, 16, 16, 256, lambda n: n % 16, lambda n: n // 16, same)
    band(w2, b2, 16, 16, 16, 256, lambda n: n % 16, lambda n: 2 * ((n // 16) % 8) + n // 128, same)

    dev = lax.axis_index("dev")

    def near(zin, z):
        at = 2 * dev - 1 + z
        return jnp.where((at >= 0) & (at < 8), zin - at + 1, -1)

    band(w3, b3, 16, 32, 8, 128, lambda n: n % 32, lambda n: n // 32, near)
    band(w4, b4, 32, 32, 4, 128, lambda n: n // 2, lambda n: n % 2, lambda zin, z: zin - z)


def taps(rows, band_ref):
    lanes = band_ref.shape[1] // 3
    size = rows[0].shape[0]
    acc = jnp.dot(jnp.concatenate(rows, axis=1), band_ref[...], preferred_element_type=F32)
    total = pltpu.roll(acc[:, :lanes], 1, 0) + acc[:, lanes : 2 * lanes] + pltpu.roll(acc[:, 2 * lanes :], size - 1, 0)
    return jnp.maximum(total, 0.0)


def place():
    tile = lax.axis_index("gx") * lax.axis_size("dev") + lax.axis_index("dev")
    gy = lax.axis_index("gy")
    last_tile = lax.axis_size("gx") * lax.axis_size("dev") - 1
    return tile, last_tile, gy, lax.axis_size("gy") - 1


def halved(cells, wide):
    size = cells.shape[0]
    wide[0:size, :] = jnp.maximum(cells[:, :128], cells[:, 128:])
    return jnp.maximum(wide[pl.ds(0, size // 2, stride=2), :], wide[pl.ds(1, size // 2, stride=2), :])


def early_kernel(to_a, to_b, b1, level):
    odd = lax.axis_index("dev") % 2
    for q in range(2):
        @pl.when(odd == 0)
        def _():
            rows = [to_b[q], to_b[1] if q == 0 else to_a[0], to_a[q]]
            level[q] = taps(rows, b1).astype(BF16)

        @pl.when(odd == 1)
        def _():
            rows = [to_a[q], to_a[1] if q == 0 else to_b[0], to_b[q]]
            level[q] = taps(rows, b1).astype(BF16)


def centre_kernel(from_b, from_a, to_a, to_b, early, b1, b2, pooled, x, level, wide):
    tile, last_tile, gy, last_gy = place()
    for at, part in row_parts(from_a, from_b, to_a, to_b):
        x[pl.ds(at, 2)] = part[...]
    for q in range(6):
        level[q] = early[q - 2] if q in (2, 3) else taps([x[q], x[q + 1], x[q + 2]], b1).astype(BF16)

    @pl.when(tile == 0)
    def _():
        level[0] = jnp.zeros((COLS, 256), BF16)

    @pl.when(tile == last_tile)
    def _():
        level[5] = jnp.zeros((COLS, 256), BF16)

    for pair in range(2):
        two = [taps([level[q], level[q + 1], level[q + 2]], b2) for q in (2 * pair, 2 * pair + 1)]
        pooled[pair] = halved(jnp.maximum(two[0], two[1]), wide)


def strips_kernel(from_d, from_c, to_c, to_d, centre, b1, b2, pooled, x, wide):
    tile, last_tile, gy, last_gy = place()
    odd = gy % 2
    x[3 - 3 * odd] = from_c[...]
    x[3 * odd] = from_d[...]
    x[2 - odd] = to_c[...]
    x[1 + odd] = to_d[...]
    pieces = []
    for two in range(4):
        parts = [x[part, two].astype(F32) for part in range(4)]
        pieces += [part[8 * r : 8 * r + 8] for r in range(2) for part in parts]
    rows = jnp.concatenate(pieces, axis=0).astype(BF16)
    level = taps([rows[0:192], rows[32:224], rows[64:256]], b1)
    at = lax.broadcasted_iota(jnp.int32, (192, 256), 0)
    col = at % 32
    keep = ((col >= 8) | (gy > 0)) & ((col < 24) | (gy < last_gy))
    keep = keep & ((at >= 32) | (tile > 0)) & ((at < 160) | (tile < last_tile))
    level = jnp.where(keep, level, 0.0).astype(BF16)
    two = taps([level[0:128], level[32:160], level[64:192]], b2)
    row = lax.broadcasted_iota(jnp.int32, (8, 128), 0)
    for pair in range(2):
        at = 64 * pair
        strip = halved(jnp.maximum(two[at : at + 32], two[at + 32 : at + 64]), wide)
        low, high = pltpu.roll(strip[0:8], 4, 0), pltpu.roll(strip[8:16], 4, 0)
        main = centre[pair]
        parts = [
            jnp.where(gy > 0, low, 0.0),
            jnp.where(row < 2, low, main[0:8]),
            main[8:120],
            jnp.where(row < 6, main[120:128], high),
            jnp.where(gy < last_gy, high, 0.0),
        ]
        done = jnp.concatenate(parts, axis=0).astype(BF16)
        for copy in range(4):
            pooled[copy, pair] = done


def edges_kernel(group, to_a, to_b):
    odd = lax.axis_index("gx") % 2
    to_a[...] = group[3 - 3 * odd]
    to_b[...] = group[3 * odd]


def coarse_row(rows, b3, keep):
    gy, last_gy = lax.axis_index("gy"), lax.axis_size("gy") - 1
    col = lax.broadcasted_iota(jnp.int32, (HALF, 128), 0)
    inside = ((col >= HALO // 2) | (gy > 0)) & ((col < HALF - HALO // 2) | (gy < last_gy)) & keep
    return jnp.where(inside, taps(rows, b3), 0.0).astype(BF16)


def feature_row(rows, b4):
    features = taps(rows, b4)
    return jnp.transpose(features[HALO // 2 : HALO // 2 + 128], (1, 0))[:64]


def inner_kernel(group, b3, b4, level, turned):
    x = [group[part, r] for part in range(4) for r in range(2)]
    for q in range(6):
        level[q] = coarse_row([x[q], x[q + 1], x[q + 2]], b3, True)
    for q in range(4):
        turned[q] = feature_row([level[q], level[q + 1], level[q + 2]], b4)


def outer_kernel(from_b, from_a, group, inner, turned, b3, b4, out, x, level, wide):
    gx = lax.axis_index("gx")
    odd = gx % 2
    x[pl.ds(2 - 2 * odd, 2)] = from_a[...]
    x[pl.ds(2 * odd, 2)] = from_b[...]
    above = [x[0], x[1], group[0, 0], group[0, 1]]
    below = [group[3, 0], group[3, 1], x[2], x[3]]
    for q in range(2):
        level[q] = coarse_row(above[q : q + 3], b3, (gx > 0) | (q > 0))
        level[2 + q] = coarse_row(below[q : q + 3], b3, (gx < lax.axis_size("gx") - 1) | (q < 1))
    above = [level[0], level[1], inner[0], inner[1]]
    below = [inner[4], inner[5], level[2], level[3]]
    for q in range(2):
        wide[pl.ds(q, 64, stride=8), :] = feature_row(above[q : q + 3], b4)
        wide[pl.ds(6 + q, 64, stride=8), :] = feature_row(below[q : q + 3], b4)
    for q in range(4):
        wide[pl.ds(2 + q, 64, stride=8), :] = turned[q]
    out[...] = wide[...].astype(BF16)


def swap_rows(cells, first):
    groups, col_tiles, devs = (lax.axis_size(axis) for axis in ("gx", "gy", "dev"))
    pairs = []
    for low in range(first, groups * devs - 1, 2):
        for t in range(col_tiles):
            one, two = (((tile // devs) * col_tiles + t) * devs + tile % devs for tile in (low, low + 1))
            pairs += [(one, two), (two, one)]
    return lax.ppermute(cells, ("gx", "gy", "dev"), pairs)


def swap(cells, axis, first):
    pairs = []
    for low in range(first, lax.axis_size(axis) - 1, 2):
        pairs += [(low, low + 1), (low + 1, low)]
    return lax.ppermute(cells, axis, pairs)


def by_tap(weight):
    return jnp.transpose(weight, (2, 3, 4, 1, 0)).reshape(27 * weight.shape[1], weight.shape[0])


def body(volume, w_first, w_second, w_third, w_fourth):
    sds = jax.ShapeDtypeStruct
    main = sds((2, COLS, 256), BF16)
    ends = sds((4, 16, 256), BF16)
    to_a, to_b = call(
        pack_kernel, [main, main], [pltpu.VMEM((256, 4, COLS), F32), pltpu.VMEM((4, COLS, 256), BF16)], 0, 1 << 20
    )(volume.reshape(256, 4, COLS))
    from_b = swap_rows(to_b, 1)
    from_a = swap_rows(to_a, 0)

    b1, b2, b3, b4 = call(
        weights_kernel,
        [sds((768, 768), BF16), sds((768, 768), BF16), sds((384, 384), BF16), sds((384, 384), BF16)],
        [],
        0,
        4 << 20,
    )(by_tap(w_first), by_tap(w_second), by_tap(w_third), by_tap(w_fourth))

    early = call(early_kernel, sds((2, COLS, 256), BF16), [], 2 * 2 * COLS * 768 * 768, 2 << 20)(to_a, to_b, b1)
    to_c, to_d = call(ends_kernel, [ends, ends], [pltpu.VMEM((2, 4, 16, 256), BF16)], 0, 1 << 18)(
        from_b, from_a, to_a, to_b, early
    )
    from_d = swap(to_d, "gy", 1)
    from_c = swap(to_c, "gy", 0)
    centre = call(
        centre_kernel,
        sds((2, 128, 128), F32),
        [pltpu.VMEM((8, COLS, 256), BF16), pltpu.VMEM((6, COLS, 256), BF16), pltpu.VMEM((COLS, 128), F32)],
        2 * 10 * COLS * 768 * 768,
        5 << 20,
    )(from_b, from_a, to_a, to_b, early, b1, b2)
    group = call(
        strips_kernel,
        sds((4, 2, HALF, 128), BF16),
        [pltpu.VMEM((4, 4, 16, 256), BF16), pltpu.VMEM((32, 128), F32)],
        2 * 320 * 768 * 768,
        4 << 20,
    )(from_d, from_c, to_c, to_d, centre, b1, b2)
    group = lax.all_to_all(group, "dev", split_axis=0, concat_axis=0, tiled=True)
    edge = sds((2, HALF, 128), BF16)
    to_a, to_b = call(edges_kernel, [edge, edge], [], 0, 1 << 18)(group)
    from_b = swap(to_b, "gx", 1)
    from_a = swap(to_a, "gx", 0)
    inner, turned = call(
        inner_kernel, [sds((6, HALF, 128), BF16), sds((4, 64, 128), F32)], [], 2 * 10 * HALF * 384 * 384, 1 << 20
    )(group, b3, b4)
    out = call(
        outer_kernel,
        sds((512, 128), BF16),
        [pltpu.VMEM((4, HALF, 128), BF16), pltpu.VMEM((4, HALF, 128), BF16), pltpu.VMEM((512, 128), F32)],
        2 * 8 * HALF * 384 * 384,
        1 << 20,
    )(from_b, from_a, group, inner, turned, b3, b4)
    return out.reshape(32, 2, 8, 128)


def solution(mesh):
    return jax.shard_map(
        body,
        mesh=mesh,
        in_specs=(P(None, None, ("gx", "dev"), "gy"), P(), P(), P(), P()),
        out_specs=P(None, "dev", "gx", "gy"),
        check_vma=False,
    )
```

```python
import jax
import jax.numpy as jnp
from jax import lax
from jax.experimental import pallas as pl
from jax.experimental.pallas import tpu as pltpu
from jax.sharding import PartitionSpec as P

F32 = jnp.float32
BF16 = jnp.bfloat16
HALO = 16
COLS = 256
WIDE = COLS + 2 * HALO
HALF = WIDE // 2
VMEM_LIMIT = 48 * 1024 * 1024


def call(kernel, outs, scratch, flops, moved):
    return pl.pallas_call(
        kernel,
        out_shape=outs,
        scratch_shapes=scratch,
        compiler_params=pltpu.CompilerParams(vmem_limit_bytes=VMEM_LIMIT),
        cost_estimate=pl.CostEstimate(flops=flops, bytes_accessed=moved, transcendentals=0),
    )


def pack_kernel(x_ref, to_a, to_b, wide, images):
    wide[...] = x_ref[...].astype(F32)
    for r in range(4):
        image = wide[:, r, :].reshape(16, 16, COLS)
        image = jnp.transpose(image, (1, 0, 2)).reshape(256, COLS)
        images[r] = jnp.transpose(image, (1, 0)).astype(BF16)
    odd = lax.axis_index("dev") % 2
    to_a[...] = images[pl.ds(2 - 2 * odd, 2)]
    to_b[...] = images[pl.ds(2 * odd, 2)]


def row_parts(from_a, from_b, to_a, to_b):
    odd = lax.axis_index("dev") % 2
    return ((6 - 6 * odd, from_a), (6 * odd, from_b), (4 - 2 * odd, to_a), (2 + 2 * odd, to_b))


def ends_kernel(from_b, from_a, to_a, to_b, after, to_c, to_d, ends):
    for at, part in row_parts(from_a, from_b, to_a, to_b):
        low = [part[r, :16].astype(F32)[:8] for r in range(2)]
        high = [part[r, COLS - 16 :].astype(F32)[8:] for r in range(2)]
        ends[0, at // 2] = jnp.concatenate(low, axis=0).astype(BF16)
        ends[1, at // 2] = jnp.concatenate(high, axis=0).astype(BF16)
    odd = lax.axis_index("gy") % 2
    to_c[...] = ends[1 - odd]
    to_d[...] = ends[odd]


def one_hot(rows, lanes, of_lane):
    row = lax.broadcasted_iota(jnp.int32, (rows, lanes), 0)
    lane = lax.broadcasted_iota(jnp.int32, (rows, lanes), 1)
    return jnp.where(of_lane(lane) == row, 1.0, 0.0).astype(BF16)


def band(w_ref, out_ref, ins, outs, depths, lanes, o_of, z_of, tap_of):
    spread = jnp.dot(w_ref[...], one_hot(outs, lanes, o_of), preferred_element_type=F32)
    lane = lax.broadcasted_iota(jnp.int32, (ins, lanes), 1)
    z = z_of(lane)
    for zin in range(depths):
        tap = tap_of(zin, z)
        masks = [tap == a for a in range(3)]
        for b in range(3):
            for c in range(3):
                block = jnp.zeros((ins, lanes), F32)
                for a in range(3):
                    at = ((a * 3 + b) * 3 + c) * ins
                    block = jnp.where(masks[a], spread[at : at + ins], block)
                row = (b * depths + zin) * ins
                out_ref[row : row + ins, c * lanes : (c + 1) * lanes] = block.astype(BF16)


def weights_kernel(w1, w2, w3, w4, b1, b2, b3, b4):
    def same(zin, z):
        return zin - z + 1

    band(w1, b1, 16, 16, 16, 256, lambda n: n % 16, lambda n: n // 16, same)
    band(w2, b2, 16, 16, 16, 256, lambda n: n % 16, lambda n: 2 * ((n // 16) % 8) + n // 128, same)

    dev = lax.axis_index("dev")

    def near(zin, z):
        at = 2 * dev - 1 + z
        return jnp.where((at >= 0) & (at < 8), zin - at + 1, -1)

    band(w3, b3, 16, 32, 8, 128, lambda n: n % 32, lambda n: n // 32, near)
    band(w4, b4, 32, 32, 4, 128, lambda n: n // 2, lambda n: n % 2, lambda zin, z: zin - z)


def taps(rows, band_ref):
    lanes = band_ref.shape[1] // 3
    size = rows[0].shape[0]
    acc = jnp.dot(jnp.concatenate(rows, axis=1), band_ref[...], preferred_element_type=F32)
    total = pltpu.roll(acc[:, :lanes], 1, 0) + acc[:, lanes : 2 * lanes] + pltpu.roll(acc[:, 2 * lanes :], size - 1, 0)
    return jnp.maximum(total, 0.0)


def place():
    tile = lax.axis_index("gx") * lax.axis_size("dev") + lax.axis_index("dev")
    gy = lax.axis_index("gy")
    last_tile = lax.axis_size("gx") * lax.axis_size("dev") - 1
    return tile, last_tile, gy, lax.axis_size("gy") - 1


def halved(cells, wide):
    size = cells.shape[0]
    wide[0:size, :] = jnp.maximum(cells[:, :128], cells[:, 128:])
    return jnp.maximum(wide[pl.ds(0, size // 2, stride=2), :], wide[pl.ds(1, size // 2, stride=2), :])


def early_kernel(to_a, to_b, b1, level):
    odd = lax.axis_index("dev") % 2
    for q in range(2):
        @pl.when(odd == 0)
        def _():
            rows = [to_b[q], to_b[1] if q == 0 else to_a[0], to_a[q]]
            level[q] = taps(rows, b1).astype(BF16)

        @pl.when(odd == 1)
        def _():
            rows = [to_a[q], to_a[1] if q == 0 else to_b[0], to_b[q]]
            level[q] = taps(rows, b1).astype(BF16)


def centre_kernel(from_b, from_a, to_a, to_b, early, b1, b2, pooled, x, level, wide):
    tile, last_tile, gy, last_gy = place()
    for at, part in row_parts(from_a, from_b, to_a, to_b):
        x[pl.ds(at, 2)] = part[...]
    for q in range(6):
        level[q] = early[q - 2] if q in (2, 3) else taps([x[q], x[q + 1], x[q + 2]], b1).astype(BF16)

    @pl.when(tile == 0)
    def _():
        level[0] = jnp.zeros((COLS, 256), BF16)

    @pl.when(tile == last_tile)
    def _():
        level[5] = jnp.zeros((COLS, 256), BF16)

    for pair in range(2):
        two = [taps([level[q], level[q + 1], level[q + 2]], b2) for q in (2 * pair, 2 * pair + 1)]
        pooled[pair] = halved(jnp.maximum(two[0], two[1]), wide)


def strips_kernel(from_d, from_c, to_c, to_d, centre, b1, b2, pooled, x, wide):
    tile, last_tile, gy, last_gy = place()
    odd = gy % 2
    x[3 - 3 * odd] = from_c[...]
    x[3 * odd] = from_d[...]
    x[2 - odd] = to_c[...]
    x[1 + odd] = to_d[...]
    pieces = []
    for two in range(4):
        parts = [x[part, two].astype(F32) for part in range(4)]
        pieces += [part[8 * r : 8 * r + 8] for r in range(2) for part in parts]
    rows = jnp.concatenate(pieces, axis=0).astype(BF16)
    level = taps([rows[0:192], rows[32:224], rows[64:256]], b1)
    at = lax.broadcasted_iota(jnp.int32, (192, 256), 0)
    col = at % 32
    keep = ((col >= 8) | (gy > 0)) & ((col < 24) | (gy < last_gy))
    keep = keep & ((at >= 32) | (tile > 0)) & ((at < 160) | (tile < last_tile))
    level = jnp.where(keep, level, 0.0).astype(BF16)
    two = taps([level[0:128], level[32:160], level[64:192]], b2)
    row = lax.broadcasted_iota(jnp.int32, (8, 128), 0)
    for pair in range(2):
        at = 64 * pair
        strip = halved(jnp.maximum(two[at : at + 32], two[at + 32 : at + 64]), wide)
        low, high = pltpu.roll(strip[0:8], 4, 0), pltpu.roll(strip[8:16], 4, 0)
        main = centre[pair]
        parts = [
            jnp.where(gy > 0, low, 0.0),
            jnp.where(row < 2, low, main[0:8]),
            main[8:120],
            jnp.where(row < 6, main[120:128], high),
            jnp.where(gy < last_gy, high, 0.0),
        ]
        pooled[pair] = jnp.concatenate(parts, axis=0).astype(BF16)


def edges_kernel(group, to_a, to_b):
    odd = lax.axis_index("gx") % 2
    to_a[...] = group[3 - 3 * odd]
    to_b[...] = group[3 * odd]


def coarse_row(rows, b3, keep):
    gy, last_gy = lax.axis_index("gy"), lax.axis_size("gy") - 1
    col = lax.broadcasted_iota(jnp.int32, (HALF, 128), 0)
    inside = ((col >= HALO // 2) | (gy > 0)) & ((col < HALF - HALO // 2) | (gy < last_gy)) & keep
    return jnp.where(inside, taps(rows, b3), 0.0).astype(BF16)


def feature_row(rows, b4):
    features = taps(rows, b4)
    return jnp.transpose(features[HALO // 2 : HALO // 2 + 128], (1, 0))[:64]


def inner_kernel(group, b3, b4, level, turned):
    x = [group[part, r] for part in range(4) for r in range(2)]
    for q in range(6):
        level[q] = coarse_row([x[q], x[q + 1], x[q + 2]], b3, True)
    for q in range(4):
        turned[q] = feature_row([level[q], level[q + 1], level[q + 2]], b4)


def outer_kernel(from_b, from_a, group, inner, turned, b3, b4, out, x, level, wide):
    gx = lax.axis_index("gx")
    odd = gx % 2
    x[pl.ds(2 - 2 * odd, 2)] = from_a[...]
    x[pl.ds(2 * odd, 2)] = from_b[...]
    above = [x[0], x[1], group[0, 0], group[0, 1]]
    below = [group[3, 0], group[3, 1], x[2], x[3]]
    for q in range(2):
        level[q] = coarse_row(above[q : q + 3], b3, (gx > 0) | (q > 0))
        level[2 + q] = coarse_row(below[q : q + 3], b3, (gx < lax.axis_size("gx") - 1) | (q < 1))
    above = [level[0], level[1], inner[0], inner[1]]
    below = [inner[4], inner[5], level[2], level[3]]
    for q in range(2):
        wide[pl.ds(q, 64, stride=8), :] = feature_row(above[q : q + 3], b4)
        wide[pl.ds(6 + q, 64, stride=8), :] = feature_row(below[q : q + 3], b4)
    for q in range(4):
        wide[pl.ds(2 + q, 64, stride=8), :] = turned[q]
    out[...] = wide[...].astype(BF16)


def swap_rows(cells, first):
    groups, col_tiles, devs = (lax.axis_size(axis) for axis in ("gx", "gy", "dev"))
    pairs = []
    for low in range(first, groups * devs - 1, 2):
        for t in range(col_tiles):
            one, two = (((tile // devs) * col_tiles + t) * devs + tile % devs for tile in (low, low + 1))
            pairs += [(one, two), (two, one)]
    return lax.ppermute(cells, ("gx", "gy", "dev"), pairs)


def swap(cells, axis, first):
    pairs = []
    for low in range(first, lax.axis_size(axis) - 1, 2):
        pairs += [(low, low + 1), (low + 1, low)]
    return lax.ppermute(cells, axis, pairs)


def by_tap(weight):
    return jnp.transpose(weight, (2, 3, 4, 1, 0)).reshape(27 * weight.shape[1], weight.shape[0])


def body(volume, w_first, w_second, w_third, w_fourth):
    sds = jax.ShapeDtypeStruct
    main = sds((2, COLS, 256), BF16)
    ends = sds((4, 16, 256), BF16)
    to_a, to_b = call(
        pack_kernel, [main, main], [pltpu.VMEM((256, 4, COLS), F32), pltpu.VMEM((4, COLS, 256), BF16)], 0, 1 << 20
    )(volume.reshape(256, 4, COLS))
    from_b = swap_rows(to_b, 1)
    from_a = swap_rows(to_a, 0)

    b1, b2, b3, b4 = call(
        weights_kernel,
        [sds((768, 768), BF16), sds((768, 768), BF16), sds((384, 384), BF16), sds((384, 384), BF16)],
        [],
        0,
        4 << 20,
    )(by_tap(w_first), by_tap(w_second), by_tap(w_third), by_tap(w_fourth))

    early = call(early_kernel, sds((2, COLS, 256), BF16), [], 2 * 2 * COLS * 768 * 768, 2 << 20)(to_a, to_b, b1)
    to_c, to_d = call(ends_kernel, [ends, ends], [pltpu.VMEM((2, 4, 16, 256), BF16)], 0, 1 << 18)(
        from_b, from_a, to_a, to_b, early
    )
    from_d = swap(to_d, "gy", 1)
    from_c = swap(to_c, "gy", 0)
    centre = call(
        centre_kernel,
        sds((2, 128, 128), F32),
        [pltpu.VMEM((8, COLS, 256), BF16), pltpu.VMEM((6, COLS, 256), BF16), pltpu.VMEM((COLS, 128), F32)],
        2 * 10 * COLS * 768 * 768,
        5 << 20,
    )(from_b, from_a, to_a, to_b, early, b1, b2)
    pooled = call(
        strips_kernel,
        sds((2, HALF, 128), BF16),
        [pltpu.VMEM((4, 4, 16, 256), BF16), pltpu.VMEM((32, 128), F32)],
        2 * 320 * 768 * 768,
        4 << 20,
    )(from_d, from_c, to_c, to_d, centre, b1, b2)
    group = lax.all_gather(pooled, "dev")
    edge = sds((2, HALF, 128), BF16)
    to_a, to_b = call(edges_kernel, [edge, edge], [], 0, 1 << 18)(group)
    from_b = swap(to_b, "gx", 1)
    from_a = swap(to_a, "gx", 0)
    inner, turned = call(
        inner_kernel, [sds((6, HALF, 128), BF16), sds((4, 64, 128), F32)], [], 2 * 10 * HALF * 384 * 384, 1 << 20
    )(group, b3, b4)
    out = call(
        outer_kernel,
        sds((512, 128), BF16),
        [pltpu.VMEM((4, HALF, 128), BF16), pltpu.VMEM((4, HALF, 128), BF16), pltpu.VMEM((512, 128), F32)],
        2 * 8 * HALF * 384 * 384,
        1 << 20,
    )(from_b, from_a, group, inner, turned, b3, b4)
    return out.reshape(32, 2, 8, 128)


def solution(mesh):
    return jax.shard_map(
        body,
        mesh=mesh,
        in_specs=(P(None, None, ("gx", "dev"), "gy"), P(), P(), P(), P()),
        out_specs=P(None, "dev", "gx", "gy"),
        check_vma=False,
    )
```

```python
import jax
import jax.numpy as jnp
from jax import lax
from jax.experimental import pallas as pl
from jax.experimental.pallas import tpu as pltpu
from jax.sharding import PartitionSpec as P

F32 = jnp.float32
BF16 = jnp.bfloat16
HALO = 16
COLS = 256
WIDE = COLS + 2 * HALO
HALF = WIDE // 2
VMEM_LIMIT = 48 * 1024 * 1024


def call(kernel, outs, scratch, flops, moved):
    return pl.pallas_call(
        kernel,
        out_shape=outs,
        scratch_shapes=scratch,
        compiler_params=pltpu.CompilerParams(vmem_limit_bytes=VMEM_LIMIT),
        cost_estimate=pl.CostEstimate(flops=flops, bytes_accessed=moved, transcendentals=0),
    )


def pack_kernel(x_ref, to_a, to_b, wide, images):
    wide[...] = x_ref[...].astype(F32)
    for r in range(4):
        image = wide[:, r, :].reshape(16, 16, COLS)
        image = jnp.transpose(image, (1, 0, 2)).reshape(256, COLS)
        images[r] = jnp.transpose(image, (1, 0)).astype(BF16)
    odd = lax.axis_index("dev") % 2
    to_a[...] = images[pl.ds(2 - 2 * odd, 2)]
    to_b[...] = images[pl.ds(2 * odd, 2)]


def row_parts(from_a, from_b, to_a, to_b):
    odd = lax.axis_index("dev") % 2
    return ((6 - 6 * odd, from_a), (6 * odd, from_b), (4 - 2 * odd, to_a), (2 + 2 * odd, to_b))


def ends_kernel(from_b, from_a, to_a, to_b, after, to_c, to_d, ends):
    for at, part in row_parts(from_a, from_b, to_a, to_b):
        low = [part[r, :16].astype(F32)[:8] for r in range(2)]
        high = [part[r, COLS - 16 :].astype(F32)[8:] for r in range(2)]
        ends[0, at // 2] = jnp.concatenate(low, axis=0).astype(BF16)
        ends[1, at // 2] = jnp.concatenate(high, axis=0).astype(BF16)
    odd = lax.axis_index("gy") % 2
    to_c[...] = ends[1 - odd]
    to_d[...] = ends[odd]


def one_hot(rows, lanes, of_lane):
    row = lax.broadcasted_iota(jnp.int32, (rows, lanes), 0)
    lane = lax.broadcasted_iota(jnp.int32, (rows, lanes), 1)
    return jnp.where(of_lane(lane) == row, 1.0, 0.0).astype(BF16)


def band(w_ref, out_ref, ins, outs, depths, lanes, o_of, z_of, tap_of):
    spread = jnp.dot(w_ref[...], one_hot(outs, lanes, o_of), preferred_element_type=F32)
    lane = lax.broadcasted_iota(jnp.int32, (ins, lanes), 1)
    z = z_of(lane)
    for zin in range(depths):
        tap = tap_of(zin, z)
        masks = [tap == a for a in range(3)]
        for b in range(3):
            for c in range(3):
                block = jnp.zeros((ins, lanes), F32)
                for a in range(3):
                    at = ((a * 3 + b) * 3 + c) * ins
                    block = jnp.where(masks[a], spread[at : at + ins], block)
                row = (b * depths + zin) * ins
                out_ref[row : row + ins, c * lanes : (c + 1) * lanes] = block.astype(BF16)


def weights_kernel(w1, w2, w3, w4, b1, b2, b3, b4):
    def same(zin, z):
        return zin - z + 1

    band(w1, b1, 16, 16, 16, 256, lambda n: n % 16, lambda n: n // 16, same)
    band(w2, b2, 16, 16, 16, 256, lambda n: n % 16, lambda n: 2 * ((n // 16) % 8) + n // 128, same)

    dev = lax.axis_index("dev")

    def near(zin, z):
        at = 2 * dev - 1 + z
        return jnp.where((at >= 0) & (at < 8), zin - at + 1, -1)

    band(w3, b3, 16, 32, 8, 128, lambda n: n % 32, lambda n: n // 32, near)
    band(w4, b4, 32, 32, 4, 128, lambda n: n // 2, lambda n: n % 2, lambda zin, z: zin - z)


def taps(rows, band_ref):
    lanes = band_ref.shape[1] // 3
    size = rows[0].shape[0]
    acc = jnp.dot(jnp.concatenate(rows, axis=1), band_ref[...], preferred_element_type=F32)
    total = pltpu.roll(acc[:, :lanes], 1, 0) + acc[:, lanes : 2 * lanes] + pltpu.roll(acc[:, 2 * lanes :], size - 1, 0)
    return jnp.maximum(total, 0.0)


def place():
    tile = lax.axis_index("gx") * lax.axis_size("dev") + lax.axis_index("dev")
    gy = lax.axis_index("gy")
    last_tile = lax.axis_size("gx") * lax.axis_size("dev") - 1
    return tile, last_tile, gy, lax.axis_size("gy") - 1


def halved(cells, wide):
    size = cells.shape[0]
    wide[0:size, :] = jnp.maximum(cells[:, :128], cells[:, 128:])
    return jnp.maximum(wide[pl.ds(0, size // 2, stride=2), :], wide[pl.ds(1, size // 2, stride=2), :])


def early_kernel(to_a, to_b, b1, level):
    odd = lax.axis_index("dev") % 2
    for q in range(2):
        @pl.when(odd == 0)
        def _():
            rows = [to_b[q], to_b[1] if q == 0 else to_a[0], to_a[q]]
            level[q] = taps(rows, b1).astype(BF16)

        @pl.when(odd == 1)
        def _():
            rows = [to_a[q], to_a[1] if q == 0 else to_b[0], to_b[q]]
            level[q] = taps(rows, b1).astype(BF16)


def centre_kernel(from_b, from_a, to_a, to_b, early, b1, b2, pooled, x, level, wide):
    tile, last_tile, gy, last_gy = place()
    for at, part in row_parts(from_a, from_b, to_a, to_b):
        x[pl.ds(at, 2)] = part[...]
    for q in range(6):
        level[q] = early[q - 2] if q in (2, 3) else taps([x[q], x[q + 1], x[q + 2]], b1).astype(BF16)

    @pl.when(tile == 0)
    def _():
        level[0] = jnp.zeros((COLS, 256), BF16)

    @pl.when(tile == last_tile)
    def _():
        level[5] = jnp.zeros((COLS, 256), BF16)

    for pair in range(2):
        two = [taps([level[q], level[q + 1], level[q + 2]], b2) for q in (2 * pair, 2 * pair + 1)]
        pooled[pair] = halved(jnp.maximum(two[0], two[1]), wide)


def strips_kernel(from_d, from_c, to_c, to_d, centre, b1, b2, pooled, x, wide):
    tile, last_tile, gy, last_gy = place()
    odd = gy % 2
    x[3 - 3 * odd] = from_c[...]
    x[3 * odd] = from_d[...]
    x[2 - odd] = to_c[...]
    x[1 + odd] = to_d[...]
    pieces = []
    for two in range(4):
        parts = [x[part, two].astype(F32) for part in range(4)]
        pieces += [part[8 * r : 8 * r + 8] for r in range(2) for part in parts]
    rows = jnp.concatenate(pieces, axis=0).astype(BF16)
    level = taps([rows[0:192], rows[32:224], rows[64:256]], b1)
    at = lax.broadcasted_iota(jnp.int32, (192, 256), 0)
    col = at % 32
    keep = ((col >= 8) | (gy > 0)) & ((col < 24) | (gy < last_gy))
    keep = keep & ((at >= 32) | (tile > 0)) & ((at < 160) | (tile < last_tile))
    level = jnp.where(keep, level, 0.0).astype(BF16)
    two = taps([level[0:128], level[32:160], level[64:192]], b2)
    row = lax.broadcasted_iota(jnp.int32, (8, 128), 0)
    for pair in range(2):
        at = 64 * pair
        strip = halved(jnp.maximum(two[at : at + 32], two[at + 32 : at + 64]), wide)
        low, high = pltpu.roll(strip[0:8], 4, 0), pltpu.roll(strip[8:16], 4, 0)
        main = centre[pair]
        parts = [
            jnp.where(gy > 0, low, 0.0),
            jnp.where(row < 2, low, main[0:8]),
            main[8:120],
            jnp.where(row < 6, main[120:128], high),
            jnp.where(gy < last_gy, high, 0.0),
        ]
        done = jnp.concatenate(parts, axis=0).astype(BF16)
        for copy in range(4):
            pooled[copy, pair] = done


def edges_kernel(group, to_a, to_b):
    odd = lax.axis_index("gx") % 2
    to_a[...] = group[3 - 3 * odd]
    to_b[...] = group[3 * odd]


def taps_of(triples, band_ref):
    size = triples[0][0].shape[0]
    total = taps([jnp.concatenate([triple[k] for triple in triples], axis=0) for k in range(3)], band_ref)
    return [total[size * at : size * at + size] for at in range(len(triples))]


def coarse_rows(triples, b3, keeps):
    gy, last_gy = lax.axis_index("gy"), lax.axis_size("gy") - 1
    col = lax.broadcasted_iota(jnp.int32, (HALF, 128), 0)
    inside = ((col >= HALO // 2) | (gy > 0)) & ((col < HALF - HALO // 2) | (gy < last_gy))
    rows = taps_of(triples, b3)
    return [jnp.where(inside & keep, row, 0.0).astype(BF16) for row, keep in zip(rows, keeps)]


def feature_rows(triples, b4):
    rows = taps_of(triples, b4)
    return [jnp.transpose(row[HALO // 2 : HALO // 2 + 128], (1, 0))[:64] for row in rows]


def inner_kernel(group, b3, b4, level, turned):
    x = [group[part, r] for part in range(4) for r in range(2)]
    for half in range(2):
        rows = coarse_rows([x[q : q + 3] for q in range(3 * half, 3 * half + 3)], b3, [True] * 3)
        for q in range(3):
            level[3 * half + q] = rows[q]
    rows = feature_rows([[level[q], level[q + 1], level[q + 2]] for q in range(4)], b4)
    for q in range(4):
        turned[q] = rows[q]


def outer_kernel(from_b, from_a, group, inner, turned, b3, b4, out, x, wide):
    gx, last_gx = lax.axis_index("gx"), lax.axis_size("gx") - 1
    odd = gx % 2
    x[pl.ds(2 - 2 * odd, 2)] = from_a[...]
    x[pl.ds(2 * odd, 2)] = from_b[...]
    above = [x[0], x[1], group[0, 0], group[0, 1]]
    below = [group[3, 0], group[3, 1], x[2], x[3]]
    triples = [above[0:3], above[1:4], below[0:3], below[1:4]]
    level = coarse_rows(triples, b3, [gx > 0, True, True, gx < last_gx])
    above = [level[0], level[1], inner[0], inner[1]]
    below = [inner[4], inner[5], level[2], level[3]]
    rows = feature_rows([above[0:3], above[1:4], below[0:3], below[1:4]], b4)
    for row, at in zip(rows, (0, 1, 6, 7)):
        wide[pl.ds(at, 64, stride=8), :] = row
    for q in range(4):
        wide[pl.ds(2 + q, 64, stride=8), :] = turned[q]
    out[...] = wide[...].astype(BF16)


def swap_rows(cells, first):
    groups, col_tiles, devs = (lax.axis_size(axis) for axis in ("gx", "gy", "dev"))
    pairs = []
    for low in range(first, groups * devs - 1, 2):
        for t in range(col_tiles):
            one, two = (((tile // devs) * col_tiles + t) * devs + tile % devs for tile in (low, low + 1))
            pairs += [(one, two), (two, one)]
    return lax.ppermute(cells, ("gx", "gy", "dev"), pairs)


def swap(cells, axis, first):
    pairs = []
    for low in range(first, lax.axis_size(axis) - 1, 2):
        pairs += [(low, low + 1), (low + 1, low)]
    return lax.ppermute(cells, axis, pairs)


def by_tap(weight):
    return jnp.transpose(weight, (2, 3, 4, 1, 0)).reshape(27 * weight.shape[1], weight.shape[0])


def body(volume, w_first, w_second, w_third, w_fourth):
    sds = jax.ShapeDtypeStruct
    main = sds((2, COLS, 256), BF16)
    ends = sds((4, 16, 256), BF16)
    to_a, to_b = call(
        pack_kernel, [main, main], [pltpu.VMEM((256, 4, COLS), F32), pltpu.VMEM((4, COLS, 256), BF16)], 0, 1 << 20
    )(volume.reshape(256, 4, COLS))
    from_b = swap_rows(to_b, 1)
    from_a = swap_rows(to_a, 0)

    b1, b2, b3, b4 = call(
        weights_kernel,
        [sds((768, 768), BF16), sds((768, 768), BF16), sds((384, 384), BF16), sds((384, 384), BF16)],
        [],
        0,
        4 << 20,
    )(by_tap(w_first), by_tap(w_second), by_tap(w_third), by_tap(w_fourth))

    early = call(early_kernel, sds((2, COLS, 256), BF16), [], 2 * 2 * COLS * 768 * 768, 2 << 20)(to_a, to_b, b1)
    to_c, to_d = call(ends_kernel, [ends, ends], [pltpu.VMEM((2, 4, 16, 256), BF16)], 0, 1 << 18)(
        from_b, from_a, to_a, to_b, early
    )
    from_d = swap(to_d, "gy", 1)
    from_c = swap(to_c, "gy", 0)
    centre = call(
        centre_kernel,
        sds((2, 128, 128), F32),
        [pltpu.VMEM((8, COLS, 256), BF16), pltpu.VMEM((6, COLS, 256), BF16), pltpu.VMEM((COLS, 128), F32)],
        2 * 10 * COLS * 768 * 768,
        5 << 20,
    )(from_b, from_a, to_a, to_b, early, b1, b2)
    group = call(
        strips_kernel,
        sds((4, 2, HALF, 128), BF16),
        [pltpu.VMEM((4, 4, 16, 256), BF16), pltpu.VMEM((32, 128), F32)],
        2 * 320 * 768 * 768,
        4 << 20,
    )(from_d, from_c, to_c, to_d, centre, b1, b2)
    group = lax.all_to_all(group, "dev", split_axis=0, concat_axis=0, tiled=True)
    edge = sds((2, HALF, 128), BF16)
    to_a, to_b = call(edges_kernel, [edge, edge], [], 0, 1 << 18)(group)
    from_b = swap(to_b, "gx", 1)
    from_a = swap(to_a, "gx", 0)
    inner, turned = call(
        inner_kernel, [sds((6, HALF, 128), BF16), sds((4, 64, 128), F32)], [], 2 * 10 * HALF * 384 * 384, 1 << 20
    )(group, b3, b4)
    out = call(
        outer_kernel,
        sds((512, 128), BF16),
        [pltpu.VMEM((4, HALF, 128), BF16), pltpu.VMEM((512, 128), F32)],
        2 * 8 * HALF * 384 * 384,
        1 << 20,
    )(from_b, from_a, group, inner, turned, b3, b4)
    return out.reshape(32, 2, 8, 128)


def solution(mesh):
    return jax.shard_map(
        body,
        mesh=mesh,
        in_specs=(P(None, None, ("gx", "dev"), "gy"), P(), P(), P(), P()),
        out_specs=P(None, "dev", "gx", "gy"),
        check_vma=False,
    )
```
